256 devices in a mesh: prow: 8 (over z_hi, core), pcol: 32 (over x, y, z_lo).
Axes of the slice: x: 4, y: 4, z: 8 (z_hi: 4, z_lo: 2; z = z_hi * 2 + z_lo), core: 2. Of those that a mesh axis runs over, the one named last changes fastest.
Arguments:
- inverse_anc: float32 [8192, 8192], P('prow', 'pcol'), as said below
- lower_two: float32 [8192, 2048], P('prow', 'pcol'), may hold values from -1.5 to 1.5
- pattern_two: int32 [32, 8], replicated, may hold values 0 or 1
- widths_two: int32 [8], replicated, may hold values from 64 to 256
- dinv_two: float32 [8, 256, 256], P('prow'), may hold values from -6 to 6
- lower_one: float32 [8192, 2048], P('prow', 'pcol'), may hold values from -1.5 to 1.5
- pattern_one: int32 [32, 8], replicated, may hold values 0 or 1
- widths_one: int32 [8], replicated, may hold values from 64 to 256
- parent_one: int32 [8], replicated, may hold values from 0 to 7
- lower_par: float32 [8, 256, 256], P('prow'), may hold values from -0.3 to 0.3
- dinv_one: float32 [8, 256, 256], P('prow'), may hold values from -6 to 6
Outputs:
- upper_two: float32 [2048, 8192], P('prow', 'pcol')
- diag_two: float32 [8, 256, 256], P('prow')
- upper_one: float32 [2048, 8192], P('prow', 'pcol')
- parent_block: float32 [8, 256, 256], P('prow')
- diag_one: float32 [8, 256, 256], P('prow')
The draws below stay inside these ranges and needn't reach their ends.
Inputs may be any that keep to these rules, and one draw needn't show every extreme that they name: inverse_anc is symmetric.
All inputs are finite; a program needn't handle non-finite values.
Results may differ from the reference program's by a relative error of at most 0.00011.
Values sent between devices are 32-bit elements; how exact they have to be, the bound alone decides.
A program may use at most 128 MiB of HBM per device.

```python
import jax
import jax.numpy as jnp
from jax import lax

B = 256
NA = 32
NSUP = 8
M = 8192
C = 2048


def draw_inverse_anc(key, part):
    key = jax.random.fold_in(key, 11)
    first = jax.random.fold_in(key, 0)
    base = jax.random.normal(first, (M, M), jnp.float32)
    return ((base + base.T) * (1.0 / M) ** 0.5).astype(jnp.float32)


def touch_ends(entries, own_key, least, top_value):
    longest = entries.shape.index(max(entries.shape))
    spots = []
    for shift in (0, 1):
        where = [jax.random.randint(jax.random.fold_in(own_key, axis), (), 0, length) for axis, length in enumerate(entries.shape)]
        where[longest] = (where[longest] + shift) % entries.shape[longest]
        spots.append(tuple(where))
    return entries.at[spots[0]].set(least).at[spots[1]].set(top_value)


def steps_of(stream_key, dims, shards, low, top_value):
    factor_of, own = 1.0, jax.random.fold_in(stream_key, 6)
    for position, shards_of in shards:
        steps = jnp.exp(jax.random.uniform(jax.random.fold_in(own, position), (shards_of,), jnp.float32, low / len(shards), top_value / len(shards)))
        factor_of = factor_of * jnp.repeat(steps, dims[position] // shards_of).reshape([-1 if axis == position else 1 for axis in range(len(dims))])
    return factor_of


def scatter_about(rng, dims, spread, most, shards=(), kind=jnp.bfloat16):
    factor_of = steps_of(rng, dims, shards, -0.22, 0.18) if shards else 1.0
    result = jax.random.normal(rng, dims, jnp.float32) * spread * factor_of
    return jnp.minimum(jnp.maximum(result, -most), most).astype(kind)


def setup_inputs(seed: int = 0) -> dict:
    splits = jax.random.split(jax.random.key(seed), 12)
    inverse_anc = draw_inverse_anc(jax.random.fold_in(splits[11], 71), 0)
    lower_two = scatter_about(splits[1], (M, C), 0.25, 1.5, ((0, 8), (1, 32)), jnp.float32)
    pattern_two = touch_ends((jax.random.randint(splits[2], (NA, NSUP), 0, 2) < 1).astype(jnp.int32), jax.random.fold_in(splits[2], 1), 0, 1)
    widths_two = touch_ends(jax.random.randint(splits[3], (NSUP,), B // 4, B + 1), jax.random.fold_in(splits[3], 1), B // 4, B).astype(jnp.int32)
    dinv_two = scatter_about(splits[4], (NSUP, B, B), 1.0, 6.0, ((0, 8),), jnp.float32)
    lower_one = scatter_about(splits[5], (M, C), 0.25, 1.5, ((0, 8), (1, 32)), jnp.float32)
    pattern_one = touch_ends((jax.random.randint(splits[6], (NA, NSUP), 0, 2) < 1).astype(jnp.int32), jax.random.fold_in(splits[6], 1), 0, 1)
    widths_one = touch_ends(jax.random.randint(splits[7], (NSUP,), B // 4, B + 1), jax.random.fold_in(splits[7], 1), B // 4, B).astype(jnp.int32)
    parent_one = touch_ends(jax.random.randint(splits[8], (NSUP,), 0, NSUP), jax.random.fold_in(splits[8], 1), 0, NSUP - 1).astype(jnp.int32)
    lower_par = scatter_about(splits[9], (NSUP, B, B), 0.05, 0.3, ((0, 8),), jnp.float32)
    dinv_one = scatter_about(splits[10], (NSUP, B, B), 1.0, 6.0, ((0, 8),), jnp.float32)
    return {"inverse_anc": inverse_anc, "lower_two": lower_two, "pattern_two": pattern_two, "widths_two": widths_two, "dinv_two": dinv_two, "lower_one": lower_one, "pattern_one": pattern_one, "widths_one": widths_one, "parent_one": parent_one, "lower_par": lower_par, "dinv_one": dinv_one}


HIGH = lax.Precision.HIGHEST


def column_mask(pattern, widths):
    count = pattern.shape[1]
    blocks = jnp.repeat(jnp.repeat(pattern.astype(jnp.float32), B, axis=0), B, axis=1)
    inner = jnp.arange(count * B) % B
    owner = jnp.arange(count * B) // B
    keep = (inner < widths[owner]).astype(jnp.float32)
    return blocks * keep[None, :]


def reference(inverse_anc, lower_two, pattern_two, widths_two, dinv_two, lower_one, pattern_one, widths_one, parent_one, lower_par, dinv_one):
    lmat_two = lower_two * column_mask(pattern_two, widths_two)
    xmat_two = -jnp.dot(inverse_anc, lmat_two, precision=HIGH, preferred_element_type=jnp.float32)
    l2b = lmat_two.reshape(M, NSUP, B)
    x2b = xmat_two.reshape(M, NSUP, B)
    diag_two = dinv_two - jnp.einsum('inb,inc->nbc', l2b, x2b, precision=HIGH)
    lmat_one = lower_one * column_mask(pattern_one, widths_one)
    l1b = lmat_one.reshape(M, NSUP, B)
    inner = jnp.arange(B)
    row_keep = (inner[None, :] < widths_two[parent_one][:, None]).astype(jnp.float32)
    col_keep = (inner[None, :] < widths_one[:, None]).astype(jnp.float32)
    lpar = lower_par * row_keep[:, :, None] * col_keep[:, None, :]
    xpar = x2b[:, parent_one, :]
    main = jnp.dot(inverse_anc, lmat_one, precision=HIGH, preferred_element_type=jnp.float32).reshape(M, NSUP, B)
    x1b = -main - jnp.einsum('inb,nbc->inc', xpar, lpar, precision=HIGH)
    parent_block = -jnp.einsum('inb,inc->nbc', xpar, l1b, precision=HIGH) - jnp.einsum('nbc,ncd->nbd', diag_two[parent_one], lpar, precision=HIGH)
    diag_one = dinv_one - jnp.einsum('inb,inc->nbc', l1b, x1b, precision=HIGH) - jnp.einsum('nbc,nbd->ncd', lpar, parent_block, precision=HIGH)
    upper_two = xmat_two.T
    upper_one = x1b.reshape(M, NSUP * B).T
    return (upper_two, diag_two, upper_one, parent_block, diag_one)
```

```python
import functools

import jax
import jax.numpy as jnp
from jax import lax
from jax.experimental import pallas as pl
from jax.experimental.pallas import tpu as pltpu
from jax.sharding import PartitionSpec as P

B = 256
MESH = pl.DeviceIdType.MESH
F32 = jnp.float32
BF16 = jnp.bfloat16
NN = (((1,), (0,)), ((), ()))
NT = (((1,), (1,)), ((), ()))
SEMS = 80


def split(value):
    high = value.astype(BF16)
    return high, (value - high.astype(F32)).astype(BF16)


def mm(left, right, dims=NN):
    lh, ll = split(left)
    rh, rl = split(right)
    dot = functools.partial(lax.dot_general, dimension_numbers=dims, preferred_element_type=F32)
    return dot(lh, rh) + (dot(lh, rl) + dot(ll, rh))


def kernel(
    par, a, lt, lpt, d2, d1,
    u2, u1, g2o, pbo, g1o,
    ag, lg, lh, ll, ah, al, pp, rc, r_in, pl_in, f_in, s_out,
    lloc, lsnd, lpn, d2s, x2all, l2all, x1, red, ry, yr, rz, zr, gz, fin,
    send_sem, recv_sem,
):
    r, q = lax.axis_index("prow"), lax.axis_index("pcol")
    k, c = lax.div(r, 2), lax.rem(r, 2)
    h, y, w = lax.div(q, 8), lax.rem(lax.div(q, 2), 4), lax.rem(q, 2)
    zi = 2 * k + w
    oc = 1 - c
    n = 2 * h + c

    def dev(k=k, c=c, h=h, y=y, w=w):
        return (2 * k + c, 8 * h + 2 * y + w)

    def ring(v, off, size=4):
        return lax.rem(v + (off + size), size)

    def zdev(v):
        return dev(k=lax.div(v, 2), w=lax.rem(v, 2))

    ids = [0]
    pending = []

    def copy(src, dst, device, recv=None, start=True, keep=True):
        num = ids[0]
        ids[0] += 1
        op = pltpu.make_async_remote_copy(
            src_ref=src,
            dst_ref=dst,
            send_sem=send_sem.at[num],
            recv_sem=recv_sem.at[num if recv is None else recv],
            device_id=device,
            device_id_type=MESH,
        )
        if start:
            op.start()
        if keep:
            pending.append(op)
        return op

    barrier = pltpu.get_barrier_semaphore()
    friends = [dev(c=oc)]
    friends += [dev(h=ring(h, o)) for o in (1, 2, 3)]
    friends += [dev(y=ring(y, o)) for o in (1, 2, 3)]
    friends += [zdev(ring(zi, o, 8)) for o in range(1, 8)]
    for friend in friends:
        pl.semaphore_signal(barrier, inc=1, device_id=friend, device_id_type=MESH)

    @pl.when(h != k)
    def _():
        pl.semaphore_signal(barrier, inc=1, device_id=dev(k=h, h=k), device_id_type=MESH)

    pl.semaphore_wait(barrier, len(friends) + jnp.where(h != k, 1, 0))

    hl, hr = dev(h=ring(h, -1)), dev(h=ring(h, 1))
    yl, yr_dev = dev(y=ring(y, -1)), dev(y=ring(y, 1))
    sib = dev(c=oc)
    mine = 2 * y + w
    theirs = 2 * y + 1 - w
    top, bot = pl.ds(0, 512), pl.ds(512, 512)

    lw = copy(lt, lg.at[mine], dev(w=1 - w))
    a_rt = copy(a.at[top], ag.at[0, top], hr)
    a_lb = copy(a.at[bot], ag.at[1, bot], hl)
    l_r0 = copy(lt, lg.at[mine], yr_dev)
    l_l0 = copy(lt, lg.at[mine], yl)
    a_rb = copy(a.at[bot], ag.at[0, bot], hr)
    a_lt = copy(a.at[top], ag.at[1, top], hl)
    lg[mine] = lt[...]
    d2c = copy(d2, d2s, sib)

    lp_recv = ids[0]
    lp_ops = [
        copy(lpt, lpn, dev(k=ring(k, o)), recv=lp_recv, start=False, keep=False) for o in (1, 2, 3)
    ]

    @pl.when(h == k)
    def _():
        lpn[...] = lpt[...]
        for op in lp_ops:
            op.start()

    def split_l(m):
        hi, lo = split(lg[m].reshape(128, 1024))
        lh[m] = hi
        ll[m] = lo

    split_l(mine)
    lw.wait_recv()
    l_r1 = copy(lg.at[theirs], lg.at[theirs], yr_dev)
    l_l1 = copy(lg.at[theirs], lg.at[theirs], yl)
    split_l(theirs)
    a_rt.wait_recv()
    a_fr = copy(ag.at[0, top], ag.at[2, top], hr)
    a_lb.wait_recv()
    a_fl = copy(ag.at[1, bot], ag.at[2, bot], hl)
    from_l, from_r = ring(y, -1), ring(y, 1)
    l_r0.wait_recv()
    m0 = 2 * from_l + w
    l_f0 = copy(lg.at[m0, 0], lg.at[m0, 0], yr_dev)
    l_l0.wait_recv()
    m1 = 2 * from_r + w
    l_f1 = copy(lg.at[m1, 1], lg.at[m1, 1], yl)
    split_l(m0)
    split_l(m1)
    l_r1.wait_recv()
    m2 = 2 * from_l + 1 - w
    l_f2 = copy(lg.at[m2, 0], lg.at[m2, 0], yr_dev)
    l_l1.wait_recv()
    m3 = 2 * from_r + 1 - w
    l_f3 = copy(lg.at[m3, 1], lg.at[m3, 1], yl)
    split_l(m2)
    split_l(m3)
    far = ring(y, 2)
    l_f0.wait_recv()
    l_f1.wait_recv()
    split_l(2 * far + w)
    l_f2.wait_recv()
    l_f3.wait_recv()
    split_l(2 * far + 1 - w)

    cy = lax.div(y, 2)
    off = pl.multiple_of(lax.rem(mine, 4) * B, B)
    l_op = copy(lsnd, lloc, sib, start=False, keep=False)

    @pl.when(c == cy)
    def _():
        for lev in range(2):
            lsnd[lev] = lg[pl.ds(4 * oc, 4), lev, :, pl.ds(off, B)].reshape(B, B)
        l_op.start()
        for lev in range(2):
            lloc[lev] = lg[pl.ds(4 * c, 4), lev, :, pl.ds(off, B)].reshape(B, B)

    @pl.when(c != cy)
    def _():
        l_op.wait_recv()

    def gather_x(buf):
        return [copy(buf.at[n], buf.at[n], dev(h=ring(h, o))) for o in (1, 2, 3)] + [
            copy(buf.at[n], buf.at[n], sib)
        ]

    def gather_sib(buf, ops):
        out = [ops[3]]
        for o in (1, 2, 3):
            ops[o - 1].wait_recv()
            slot = 2 * ring(h, -o) + c
            out.append(copy(buf.at[slot], buf.at[slot], sib))
        return out

    l2all[n] = lloc[0]
    l2_ops = gather_x(l2all)

    def product(parity):
        left_h = lh[pl.ds(4 * parity, 4)].reshape(512, 1024)
        left_l = ll[pl.ds(4 * parity, 4)].reshape(512, 1024)
        dot = functools.partial(lax.dot_general, dimension_numbers=NN, preferred_element_type=F32)
        return dot(left_h, ah[...]) + (dot(left_h, al[...]) + dot(left_l, ah[...]))

    def store(slot, parity, value):
        for quarter in range(4):
            for lev in range(2):
                base = quarter * 128 + lev * 64
                pp[slot, parity, lev, quarter * 64 : quarter * 64 + 64, :] = value[base : base + 64]

    def add_sib(slot, op):
        op.wait_recv()
        for lev in range(2):
            pp[slot, c, lev] += rc[slot, lev]

    blocks = [
        (a, 0, ()),
        (ag.at[0], -1, (a_rb,)),
        (ag.at[1], 1, (a_lt,)),
        (ag.at[2], 2, (a_fr, a_fl)),
    ]
    last = None
    for ref, rel, waits in blocks:
        for op in waits:
            op.wait_recv()
        hi, lo = split(ref[...])
        ah[...] = hi
        al[...] = lo
        slot = ring(h, rel)
        store(slot, oc, product(oc))
        op = copy(pp.at[slot, oc], rc.at[slot], sib)
        store(slot, c, product(c))
        if last is not None:
            add_sib(*last)
        last = (slot, op)
    add_sib(*last)

    kp, km, ko = ring(k, 1), ring(k, -1), ring(k, 2)
    zp, zm = dev(k=kp), dev(k=km)
    up, dn = pl.ds(0, 128), pl.ds(128, 128)
    first = []
    for lev in range(2):
        first.append(
            (
                copy(pp.at[ko, c, lev, up], r_in.at[lev, 0], zp),
                copy(pp.at[ko, c, lev, dn], r_in.at[lev, 1], zm),
                copy(pp.at[kp, c, lev, dn], pl_in.at[lev, 0], zp),
                copy(pp.at[km, c, lev, up], pl_in.at[lev, 1], zm),
            )
        )
    second = []
    for lev in range(2):
        first[lev][0].wait_recv()
        s_out[lev, 0] = r_in[lev, 0] + pp[kp, c, lev, up]
        one = copy(s_out.at[lev, 0], f_in.at[lev, 0], zp)
        first[lev][1].wait_recv()
        s_out[lev, 1] = r_in[lev, 1] + pp[km, c, lev, dn]
        two = copy(s_out.at[lev, 1], f_in.at[lev, 1], zm)
        second.append((one, two))

    l2_sib = gather_sib(l2all, l2_ops)

    def total(lev):
        first[lev][2].wait_recv()
        first[lev][3].wait_recv()
        second[lev][0].wait_recv()
        second[lev][1].wait_recv()
        upper = pp[k, c, lev, up] + f_in[lev, 0] + pl_in[lev, 1]
        lower = pp[k, c, lev, dn] + f_in[lev, 1] + pl_in[lev, 0]
        return jnp.concatenate([upper, lower], axis=0)

    x2all[n] = -total(0)
    x2_ops = gather_x(x2all)
    u2_op = copy(x2all.at[n], u2, dev(k=h, h=k), start=False, keep=False)
    u1_op = copy(x1, u1, dev(k=h, h=k), start=False, keep=False)

    @pl.when(h != k)
    def _():
        u2_op.start()

    @pl.when(h == k)
    def _():
        u2[...] = x2all[n]

    red[0] = mm(lloc[0], x2all[n], NT)
    for op in l2_sib:
        op.wait_recv()

    @pl.when(h != k)
    def _():
        lp_ops[0].wait_recv()

    parent = par[n]
    lp_here = lpn[...]
    l1p = lloc[1] - mm(lp_here, l2all[parent])
    d2c.wait_recv()
    rows = pl.ds(pl.multiple_of(mine * 32, 32), 32)
    here = jnp.where(parent == r, 1.0, 0.0)
    beside = jnp.where(parent == 2 * k + oc, 1.0, 0.0)
    own_rows = mm(d2[rows] * here + d2s[rows] * beside, lp_here, NT)
    main1 = total(1)
    for op in gather_sib(x2all, x2_ops):
        op.wait_recv()
    x2p = x2all[parent]
    x1[...] = -main1 - mm(lp_here, x2p)

    @pl.when(h != k)
    def _():
        u1_op.start()

    @pl.when(h == k)
    def _():
        u1[...] = x1[...]

    red[1] = mm(x2p, l1p, NT)
    red[1, rows] += own_rows
    red[2] = mm(lloc[1], x1[...], NT)

    y_ops = []
    for o in (1, 2, 3):
        to = ring(y, o)
        part = pl.ds(pl.multiple_of(to * 64, 64), 64)
        y_ops.append(copy(red.at[:, part], ry.at[o - 1], dev(y=to)))
    acc = red[:, pl.ds(pl.multiple_of(y * 64, 64), 64), :]
    for o in range(3):
        y_ops[o].wait_recv()
        acc = acc + ry[o]
    yr[...] = acc
    z_ops = []
    for o in range(1, 8):
        to = ring(zi, o, 8)
        part = pl.ds(pl.multiple_of(to * 8, 8), 8)
        z_ops.append(copy(yr.at[:, part], rz.at[o - 1], zdev(to)))
    own = pl.ds(pl.multiple_of(zi * 8, 8), 8)
    acc = yr[:, own, :]
    for o in range(7):
        z_ops[o].wait_recv()
        acc = acc + rz[o]
    zr[...] = acc

    base = ids[0]
    ids[0] += 8
    g_ops = [
        copy(zr, gz.at[:, own], dev(k=h, w=v), recv=base + zi, start=False, keep=False)
        for v in (0, 1)
    ]
    for v in (0, 1):

        @pl.when(2 * h + v != zi)
        def _(v=v):
            g_ops[v].start()

    x_recv = ids[0]
    x_ops = [
        copy(gz, gz, dev(h=ring(h, o)), recv=x_recv, start=False, keep=False) for o in (1, 2, 3)
    ]

    @pl.when(h == k)
    def _():
        gz[:, own, :] = zr[...]
        for o in range(1, 8):
            frm = ring(zi, o, 8)
            pltpu.make_async_remote_copy(
                src_ref=zr,
                dst_ref=gz.at[:, pl.ds(pl.multiple_of(frm * 8, 8), 8)],
                send_sem=send_sem.at[base],
                recv_sem=recv_sem.at[base + frm],
                device_id=sib,
                device_id_type=MESH,
            ).wait_recv()
        for op in x_ops:
            op.start()

    @pl.when(h != k)
    def _():
        x_ops[0].wait_recv()

    part = pl.ds(pl.multiple_of(y * 64, 64), 64)
    f_ops = [copy(gz, fin.at[:, part], dev(y=ring(y, o))) for o in (1, 2, 3)]
    fin[:, part, :] = gz[...]
    for op in f_ops:
        op.wait_recv()
    g2o[...] = d2[...] - fin[0]
    pb = -fin[1]
    pbo[...] = pb
    g1o[...] = d1[...] - fin[2] - mm(lpt[...], pb)

    @pl.when(h != k)
    def _():
        u2_op.wait()
        u1_op.wait()

    @pl.when(h == k)
    def _():
        for op in lp_ops + x_ops:
            op.wait_send()

    @pl.when(c == cy)
    def _():
        l_op.wait_send()

    for v in (0, 1):

        @pl.when(2 * h + v != zi)
        def _(v=v):
            g_ops[v].wait_send()

    for op in pending:
        op.wait_send()
    assert ids[0] <= SEMS


def masked(lower, pattern, widths, row_index, col_index):
    rows_dev, cols_dev = lower.shape
    nblocks = rows_dev // B
    first = col_index * cols_dev
    owner = first // B
    pat = lax.dynamic_slice(pattern, (row_index * nblocks, owner), (nblocks, 1))
    width = lax.dynamic_slice(widths, (owner,), (1,))
    inner = first % B + jnp.arange(cols_dev, dtype=jnp.int32)
    keep = (inner < width).astype(F32)
    block = jnp.repeat(pat[:, 0].astype(F32), B)
    return lower.T * keep[:, None] * block[None, :]


def per_device(
    inverse_anc,
    lower_two,
    pattern_two,
    widths_two,
    dinv_two,
    lower_one,
    pattern_one,
    widths_one,
    parent_one,
    lower_par,
    dinv_one,
):
    row_index = lax.axis_index("prow")
    col_index = lax.axis_index("pcol")
    lt = jnp.stack(
        [
            masked(lower_two, pattern_two, widths_two, row_index, col_index),
            masked(lower_one, pattern_one, widths_one, row_index, col_index),
        ]
    )
    parent = lax.dynamic_slice(parent_one, (row_index,), (1,))
    parent_width = jnp.sum(jnp.where(jnp.arange(8, dtype=jnp.int32) == parent, widths_two, 0))
    own_width = lax.dynamic_slice(widths_one, (row_index,), (1,))
    inner = jnp.arange(B, dtype=jnp.int32)
    lpt = (
        lower_par[0].T
        * (inner[None, :] < parent_width).astype(F32)
        * (inner[:, None] < own_width).astype(F32)
    )
    vmem = pl.BlockSpec(memory_space=pltpu.VMEM)
    square = jax.ShapeDtypeStruct((B, B), F32)
    outs = pl.pallas_call(
        kernel,
        out_shape=[square] * 5,
        in_specs=[pl.BlockSpec(memory_space=pltpu.SMEM)] + [vmem] * 5,
        out_specs=[vmem] * 5,
        scratch_shapes=[
            pltpu.VMEM((3, 1024, B), F32),
            pltpu.VMEM((8, 2, 64, 1024), F32),
            pltpu.VMEM((8, 128, 1024), BF16),
            pltpu.VMEM((8, 128, 1024), BF16),
            pltpu.VMEM((1024, B), BF16),
            pltpu.VMEM((1024, B), BF16),
            pltpu.VMEM((4, 2, 2, B, B), F32),
            pltpu.VMEM((4, 2, B, B), F32),
            pltpu.VMEM((2, 2, 128, B), F32),
            pltpu.VMEM((2, 2, 128, B), F32),
            pltpu.VMEM((2, 2, 128, B), F32),
            pltpu.VMEM((2, 2, 128, B), F32),
            pltpu.VMEM((2, B, B), F32),
            pltpu.VMEM((2, B, B), F32),
            pltpu.VMEM((B, B), F32),
            pltpu.VMEM((B, B), F32),
            pltpu.VMEM((8, B, B), F32),
            pltpu.VMEM((8, B, B), F32),
            pltpu.VMEM((B, B), F32),
            pltpu.VMEM((3, B, B), F32),
            pltpu.VMEM((3, 3, 64, B), F32),
            pltpu.VMEM((3, 64, B), F32),
            pltpu.VMEM((7, 3, 8, B), F32),
            pltpu.VMEM((3, 8, B), F32),
            pltpu.VMEM((3, 64, B), F32),
            pltpu.VMEM((3, B, B), F32),
            pltpu.SemaphoreType.DMA((SEMS,)),
            pltpu.SemaphoreType.DMA((SEMS,)),
        ],
        compiler_params=pltpu.CompilerParams(
            collective_id=0, has_side_effects=True, vmem_limit_bytes=56 * 1024 * 1024
        ),
    )(parent_one, inverse_anc, lt, lpt, dinv_two[0], dinv_one[0])
    u2, u1, g2, pb, g1 = outs
    return u2, g2[None], u1, pb[None], g1[None]


def solution(mesh):
    in_specs = (
        P("prow", "pcol"),
        P("prow", "pcol"),
        P(),
        P(),
        P("prow", None, None),
        P("prow", "pcol"),
        P(),
        P(),
        P(),
        P("prow", None, None),
        P("prow", None, None),
    )
    out_specs = (
        P("prow", "pcol"),
        P("prow", None, None),
        P("prow", "pcol"),
        P("prow", None, None),
        P("prow", None, None),
    )
    return jax.shard_map(
        per_device, mesh=mesh, in_specs=in_specs, out_specs=out_specs, check_vma=False
    )
```

```python
import functools

import jax
import jax.numpy as jnp
from jax import lax
from jax.experimental import pallas as pl
from jax.experimental.pallas import tpu as pltpu
from jax.sharding import PartitionSpec as P

B = 256
MESH = pl.DeviceIdType.MESH
F32 = jnp.float32
BF16 = jnp.bfloat16
NN = (((1,), (0,)), ((), ()))
NT = (((1,), (1,)), ((), ()))
SEMS = 160


def split(value):
    high = value.astype(BF16)
    return high, (value - high.astype(F32)).astype(BF16)


def dot3(lh, ll, rh, rl, dims=NN):
    dot = functools.partial(lax.dot_general, dimension_numbers=dims, preferred_element_type=F32)
    return dot(lh, rh) + (dot(lh, rl) + dot(ll, rh))


def mm(left, right, dims=NN):
    return dot3(*split(left), *split(right), dims)


def kernel(
    par, wid2, wid1, pat2, pat1, a, low2, low1, lpar, d2, d1,
    u2, u1, g2o, pbo, g1o,
    ag, lt, lg, lh, ll, ah, al, pp, rc, r_in, pl_in, f_in, s_out,
    lloc, lsnd, lpt, lpn, d2s, x2all, l2all, x1, t_z, t_x,
    red_a, ry_a, yr_a, rz_a, zr_a, gz_a, fin_a,
    red_b, ry_b, yr_b, rz_b, zr_b, gz_b, fin_b,
    send_sem, recv_sem,
):
    r, q = lax.axis_index("prow"), lax.axis_index("pcol")
    k, c = lax.div(r, 2), lax.rem(r, 2)
    h, y, w = lax.div(q, 8), lax.rem(lax.div(q, 2), 4), lax.rem(q, 2)
    zi = 2 * k + w
    oc = 1 - c
    n = 2 * h + c

    def dev(k=k, c=c, h=h, y=y, w=w):
        return (2 * k + c, 8 * h + 2 * y + w)

    def ring(v, off, size=4):
        return lax.rem(v + (off + size), size)

    def zdev(v):
        return dev(k=lax.div(v, 2), w=lax.rem(v, 2))

    ids = [0]
    pending = []

    def take(count):
        ids[0] += count
        return ids[0] - count

    def copy(src, dst, device, recv=None, start=True):
        num = take(1)
        op = pltpu.make_async_remote_copy(
            src_ref=src,
            dst_ref=dst,
            send_sem=send_sem.at[num],
            recv_sem=recv_sem.at[num if recv is None else recv],
            device_id=device,
            device_id_type=MESH,
        )
        if start:
            op.start()
            pending.append(op)
        return op

    def arrival(dst, recv):
        return pltpu.make_async_remote_copy(
            src_ref=dst,
            dst_ref=dst,
            send_sem=send_sem.at[0],
            recv_sem=recv_sem.at[recv],
            device_id=dev(c=oc),
            device_id_type=MESH,
        )

    barrier = pltpu.get_barrier_semaphore()
    friends = [dev(c=oc)]
    friends += [dev(h=ring(h, o)) for o in (1, 2, 3)]
    friends += [dev(y=ring(y, o)) for o in (1, 2, 3)]
    friends += [zdev(ring(zi, o, 8)) for o in range(1, 8)]
    for friend in friends:
        pl.semaphore_signal(barrier, inc=1, device_id=friend, device_id_type=MESH)

    owner = lax.div(q, 4)
    inner = lax.rem(q, 4) * 64 + lax.broadcasted_iota(jnp.int32, (64, 1024), 0)
    block = lax.broadcasted_iota(jnp.int32, (64, 1024), 1) // B
    for lev, (low, pat, wid) in enumerate(((low2, pat2, wid2), (low1, pat1, wid1))):
        present = jnp.zeros((64, 1024), F32)
        for b in range(4):
            there = pat[4 * r + b, owner].astype(F32)
            present = jnp.where(block == b, there, present)
        keep = jnp.where(inner < wid[owner], present, 0.0)
        lt[lev] = low[...].T * keep
    row = lax.broadcasted_iota(jnp.int32, (B, B), 0)
    col = lax.broadcasted_iota(jnp.int32, (B, B), 1)
    inside = jnp.where(row < wid1[r], 1.0, 0.0) * jnp.where(col < wid2[par[r]], 1.0, 0.0)
    lpt[...] = lpar[0].T * inside

    pl.semaphore_wait(barrier, len(friends))

    hl, hr = dev(h=ring(h, -1)), dev(h=ring(h, 1))
    yl, yr = dev(y=ring(y, -1)), dev(y=ring(y, 1))
    sib, pair = dev(c=oc), dev(w=1 - w)
    mine = 2 * y + w
    theirs = 2 * y + 1 - w
    ml, mr, mf = 2 * ring(y, -1), 2 * ring(y, 1), 2 * ring(y, 2)
    top, bot = pl.ds(0, 512), pl.ds(512, 512)

    def split_l(lev, m):
        hi, lo = split(lg[lev, m])
        lh[lev, m] = hi
        ll[lev, m] = lo

    def send_own(lev):
        return (
            copy(lt.at[lev], lg.at[lev, mine], yr),
            copy(lt.at[lev], lg.at[lev, mine], yl),
        )

    def send_pair(lev):
        return (
            copy(lg.at[lev, theirs], lg.at[lev, theirs], yr),
            copy(lg.at[lev, theirs], lg.at[lev, theirs], yl),
        )

    def forward_l(lev, ops, which):
        near, far = pl.ds(0, 32), pl.ds(32, 32)
        ops[0].wait_recv()
        one = copy(lg.at[lev, ml + which, near], lg.at[lev, ml + which, near], yr)
        ops[1].wait_recv()
        two = copy(lg.at[lev, mr + which, far], lg.at[lev, mr + which, far], yl)
        return one, two

    w2 = copy(lt.at[0], lg.at[0, mine], pair)
    o2 = send_own(0)
    a_rt = copy(a.at[top], ag.at[0, top], hr)
    a_lb = copy(a.at[bot], ag.at[1, bot], hl)
    a_rb = copy(a.at[bot], ag.at[0, bot], hr)
    a_lt = copy(a.at[top], ag.at[1, top], hl)
    d2c = copy(d2, d2s, sib)
    lg[0, mine] = lt[0]
    lg[1, mine] = lt[1]
    split_l(0, mine)
    split_l(1, mine)

    def split_a(ref, slot):
        hi, lo = split(ref[...])
        ah[slot] = hi
        al[slot] = lo

    split_a(a, 0)
    w2.wait_recv()
    p2 = send_pair(0)
    w1 = copy(lt.at[1], lg.at[1, mine], pair)
    f2 = forward_l(0, o2, w)
    split_l(0, theirs)
    split_l(0, ml + w)
    split_l(0, mr + w)
    a_rt.wait_recv()
    a_fr = copy(ag.at[0, top], ag.at[2, top], hr)
    a_lb.wait_recv()
    a_fl = copy(ag.at[1, bot], ag.at[2, bot], hl)
    e2 = forward_l(0, p2, 1 - w)
    o1 = send_own(1)
    split_l(0, ml + 1 - w)
    split_l(0, mr + 1 - w)

    lp_recv = ids[0]
    lp_ops = [copy(lpt, lpn, dev(k=ring(k, o)), recv=lp_recv, start=False) for o in (1, 2, 3)]

    @pl.when(h == k)
    def _():
        lpn[...] = lpt[...]
        for op in lp_ops:
            op.start()

    for op in f2:
        op.wait_recv()
    split_l(0, mf + w)
    w1.wait_recv()
    p1 = send_pair(1)
    split_l(1, theirs)
    for op in e2:
        op.wait_recv()
    split_l(0, mf + 1 - w)

    cy = lax.div(y, 2)
    off = pl.multiple_of(lax.rem(mine, 4) * B, B)
    l_ops = [copy(lsnd.at[lev], lloc.at[lev], sib, start=False) for lev in range(2)]

    def share(lev):
        @pl.when(c == cy)
        def _():
            lsnd[lev] = lg[lev, pl.ds(4 * oc, 4), :, pl.ds(off, B)].reshape(B, B)
            l_ops[lev].start()
            lloc[lev] = lg[lev, pl.ds(4 * c, 4), :, pl.ds(off, B)].reshape(B, B)

        @pl.when(c != cy)
        def _():
            l_ops[lev].wait_recv()

    kp, km, ko = ring(k, 1), ring(k, -1), ring(k, 2)
    zp, zm = dev(k=kp), dev(k=km)
    up, dn = pl.ds(0, 128), pl.ds(128, 128)
    rs = [
        (
            copy(pp.at[ko, lev, c, up], r_in.at[lev, 0], zp, start=False),
            copy(pp.at[ko, lev, c, dn], r_in.at[lev, 1], zm, start=False),
            copy(pp.at[kp, lev, c, dn], pl_in.at[lev, 0], zp, start=False),
            copy(pp.at[km, lev, c, up], pl_in.at[lev, 1], zm, start=False),
            copy(s_out.at[lev, 0], f_in.at[lev, 0], zp, start=False),
            copy(s_out.at[lev, 1], f_in.at[lev, 1], zm, start=False),
        )
        for lev in range(2)
    ]

    def product(lev, slot, block):
        def half(parity):
            left_h = lh[lev, pl.ds(4 * parity, 4)].reshape(B, 1024)
            left_l = ll[lev, pl.ds(4 * parity, 4)].reshape(B, 1024)
            pp[slot, lev, parity] = dot3(left_h, left_l, ah[block], al[block])

        half(oc)
        op = copy(pp.at[slot, lev, oc], rc.at[slot, lev], sib)
        half(c)
        op.wait_recv()
        pp[slot, lev, c] += rc[slot, lev]
        role = ring(slot, 4 - k)

        @pl.when(role == 2)
        def _():
            rs[lev][0].start()
            rs[lev][1].start()

        @pl.when(role == 1)
        def _():
            rs[lev][2].start()

        @pl.when(role == 3)
        def _():
            rs[lev][3].start()

    def relay(lev, slot):
        role = ring(slot, 4 - k)

        @pl.when(role == 1)
        def _():
            rs[lev][0].wait_recv()
            s_out[lev, 0] = r_in[lev, 0] + pp[slot, lev, c, up]
            rs[lev][4].start()

        @pl.when(role == 3)
        def _():
            rs[lev][1].wait_recv()
            s_out[lev, 1] = r_in[lev, 1] + pp[slot, lev, c, dn]
            rs[lev][5].start()

    s0, s1, s2, s3 = h, ring(h, -1), ring(h, 1), ring(h, 2)
    product(0, s0, 0)
    share(0)
    f1 = forward_l(1, o1, w)
    split_l(1, ml + w)
    split_l(1, mr + w)
    relay(0, s0)
    a_rb.wait_recv()
    split_a(ag.at[0], 1)
    product(0, s1, 1)
    e1 = forward_l(1, p1, 1 - w)
    split_l(1, ml + 1 - w)
    split_l(1, mr + 1 - w)
    a_lt.wait_recv()
    split_a(ag.at[1], 2)
    product(0, s2, 2)
    relay(0, s1)
    for op in f1:
        op.wait_recv()
    split_l(1, mf + w)
    for op in e1:
        op.wait_recv()
    split_l(1, mf + 1 - w)
    a_fr.wait_recv()
    a_fl.wait_recv()
    split_a(ag.at[2], 3)
    product(0, s3, 3)
    relay(0, s2)

    def gather_start(buf):
        return copy(buf.at[n], buf.at[n], hr), copy(buf.at[n], buf.at[n], hl), copy(
            buf.at[n], buf.at[n], sib
        )

    def gather_mid(buf, ops):
        left, right = 2 * ring(h, -1) + c, 2 * ring(h, 1) + c
        ops[0].wait_recv()
        one = copy(buf.at[left, up], buf.at[left, up], hr)
        sib_l = copy(buf.at[left], buf.at[left], sib)
        ops[1].wait_recv()
        two = copy(buf.at[right, dn], buf.at[right, dn], hl)
        sib_r = copy(buf.at[right], buf.at[right], sib)
        return one, two, ops[2], sib_l, sib_r

    def gather_end(buf, ops):
        opp = 2 * ring(h, 2) + c
        ops[0].wait_recv()
        ops[1].wait_recv()
        last = copy(buf.at[opp], buf.at[opp], sib)
        for op in ops[2:]:
            op.wait_recv()
        last.wait_recv()

    l2all[n] = lloc[0]
    lx = gather_start(l2all)
    product(1, s0, 0)
    relay(0, s3)
    share(1)
    product(1, s1, 1)
    relay(1, s0)
    lx = gather_mid(l2all, lx)
    product(1, s2, 2)
    relay(1, s1)
    product(1, s3, 3)
    relay(1, s2)
    gather_end(l2all, lx)

    def total(lev):
        for op in rs[lev][2:]:
            op.wait_recv()
        upper = pp[k, lev, c, up] + f_in[lev, 0] + pl_in[lev, 1]
        lower = pp[k, lev, c, dn] + f_in[lev, 1] + pl_in[lev, 0]
        return jnp.concatenate([upper, lower], axis=0)

    def place(lev, buf, out):
        z_base, x_base = take(4), take(4)
        via_z = copy(
            buf.at[up], t_z.at[lev, k], dev(k=h), recv=z_base + ring(k, 4 - h), start=False
        )
        via_x = copy(
            buf.at[dn], t_x.at[lev, h], dev(h=k), recv=x_base + ring(h, 4 - k), start=False
        )
        got_z, got_x = ids[0], ids[0] + 1
        take(2)
        on = []
        for o in (1, 2, 3):
            v = ring(k, o)
            on.append(copy(t_z.at[lev, v], out.at[up], dev(h=v), recv=got_z, start=False))
            on.append(copy(t_x.at[lev, v], out.at[dn], dev(k=v), recv=got_x, start=False))

        @pl.when(h != k)
        def _():
            via_z.start()
            via_x.start()

        @pl.when(h == k)
        def _():
            out[...] = buf[...]

        def pass_on():
            @pl.when(h == k)
            def _():
                for o in (1, 2, 3):
                    v = ring(k, o)
                    arrival(t_z.at[lev, v], z_base + o).wait_recv()
                    on[2 * o - 2].start()
                    arrival(t_x.at[lev, v], x_base + o).wait_recv()
                    on[2 * o - 1].start()

        def finish():
            @pl.when(h != k)
            def _():
                via_z.wait_send()
                via_x.wait_send()
                arrival(out.at[up], got_z).wait_recv()
                arrival(out.at[dn], got_x).wait_recv()

            @pl.when(h == k)
            def _():
                for op in on:
                    op.wait_send()

        return pass_on, finish

    x2all[n] = -total(0)
    xx = gather_start(x2all)
    relay(1, s3)
    pass_2, finish_2 = place(0, x2all.at[n], u2)
    red_a[0] = mm(lloc[0], x2all[n], NT)

    @pl.when(h != k)
    def _():
        lp_ops[0].wait_recv()

    parent = par[n]
    lp_h, lp_l = split(lpn[...])
    l1p = lloc[1] - dot3(lp_h, lp_l, *split(l2all[parent]))
    d2c.wait_recv()
    rows = pl.ds(pl.multiple_of(mine * 32, 32), 32)
    here = jnp.where(parent == r, 1.0, 0.0)
    beside = jnp.where(parent == 2 * k + oc, 1.0, 0.0)
    own_rows = dot3(*split(d2[0, rows] * here + d2s[0, rows] * beside), lp_h, lp_l, NT)
    xx = gather_mid(x2all, xx)
    pass_2()
    gather_end(x2all, xx)
    x2p = x2all[parent]
    red_a[1] = mm(x2p, l1p, NT)
    red_a[1, rows] += own_rows

    own8 = pl.ds(pl.multiple_of(zi * 8, 8), 8)
    own64 = pl.ds(pl.multiple_of(y * 64, 64), 64)

    class Chain:
        def __init__(self, red, ry, yr, rz, zr, gz, fin):
            self.bufs = (red, ry, yr, rz, zr, gz, fin)

        def y_start(self):
            red, ry = self.bufs[:2]
            self.ops = []
            for o in (1, 2, 3):
                to = ring(y, o)
                part = pl.ds(pl.multiple_of(to * 64, 64), 64)
                self.ops.append(copy(red.at[:, part], ry.at[o - 1], dev(y=to)))

        def z_start(self):
            red, ry, yr, rz = self.bufs[:4]
            acc = red[:, own64, :]
            for o in range(3):
                self.ops[o].wait_recv()
                acc = acc + ry[o]
            yr[...] = acc
            self.ops = []
            for o in range(1, 8):
                to = ring(zi, o, 8)
                part = pl.ds(pl.multiple_of(to * 8, 8), 8)
                self.ops.append(copy(yr.at[:, part], rz.at[o - 1], zdev(to)))

        def plane_start(self):
            yr, rz, zr, gz = self.bufs[2:6]
            acc = yr[:, own8, :]
            for o in range(7):
                self.ops[o].wait_recv()
                acc = acc + rz[o]
            zr[...] = acc
            self.base = take(8)
            self.sends = []
            for v in (0, 1):
                op = copy(
                    zr, gz.at[:, own8], dev(k=h, w=v), recv=self.base + zi, start=False
                )
                self.sends.append(op)

                @pl.when(2 * h + v != zi)
                def _(op=op):
                    op.start()

        def x_spread(self):
            zr, gz = self.bufs[4:6]
            got = ids[0]
            self.spread = [
                copy(gz, gz, dev(h=ring(h, o)), recv=got, start=False) for o in (1, 2, 3)
            ]

            @pl.when(h == k)
            def _():
                gz[:, own8, :] = zr[...]
                for o in range(1, 8):
                    frm = ring(zi, o, 8)
                    part = pl.ds(pl.multiple_of(frm * 8, 8), 8)
                    arrival(gz.at[:, part], self.base + frm).wait_recv()
                for op in self.spread:
                    op.start()

            @pl.when(h != k)
            def _():
                self.spread[0].wait_recv()

        def y_spread(self):
            gz, fin = self.bufs[5:]
            self.ops = [copy(gz, fin.at[:, own64], dev(y=ring(y, o))) for o in (1, 2, 3)]
            fin[:, own64, :] = gz[...]

        def finish(self):
            for op in self.ops:
                op.wait_recv()

        def drain(self):
            for v in (0, 1):

                @pl.when(2 * h + v != zi)
                def _(v=v):
                    self.sends[v].wait_send()

            @pl.when(h == k)
            def _():
                for op in self.spread:
                    op.wait_send()

    first = Chain(red_a, ry_a, yr_a, rz_a, zr_a, gz_a, fin_a)
    second = Chain(red_b, ry_b, yr_b, rz_b, zr_b, gz_b, fin_b)
    first.y_start()
    correction = dot3(lp_h, lp_l, *split(x2p))
    x1[...] = -total(1) - correction
    pass_1, finish_1 = place(1, x1, u1)
    red_b[0] = mm(lloc[1], x1[...], NT)
    second.y_start()
    first.z_start()
    second.z_start()
    first.plane_start()
    second.plane_start()
    pass_1()
    first.x_spread()
    first.y_spread()
    second.x_spread()
    second.y_spread()
    first.finish()
    g2o[...] = d2[0] - fin_a[0]
    pb = -fin_a[1]
    pbo[...] = pb
    update = d1[0] - mm(lpt[...], pb)
    second.finish()
    g1o[...] = update - fin_b[0]
    finish_2()
    finish_1()
    first.drain()
    second.drain()

    @pl.when(h == k)
    def _():
        for op in lp_ops:
            op.wait_send()

    @pl.when(c == cy)
    def _():
        for op in l_ops:
            op.wait_send()

    for lev in range(2):
        for op in rs[lev]:
            op.wait_send()
    for op in pending:
        op.wait_send()
    assert ids[0] <= SEMS


def settle(*refs):
    for src, dst in zip(refs[:5], refs[5:]):
        dst[...] = src[...].reshape(dst.shape)


def per_device(
    inverse_anc,
    lower_two,
    pattern_two,
    widths_two,
    dinv_two,
    lower_one,
    pattern_one,
    widths_one,
    parent_one,
    lower_par,
    dinv_one,
):
    vmem = pl.BlockSpec(memory_space=pltpu.VMEM)
    smem = pl.BlockSpec(memory_space=pltpu.SMEM)
    square = jax.ShapeDtypeStruct((B, B), F32)
    cube = jax.ShapeDtypeStruct((1, B, B), F32)

    def chain(count):
        return [
            pltpu.VMEM((count, B, B), F32),
            pltpu.VMEM((3, count, 64, B), F32),
            pltpu.VMEM((count, 64, B), F32),
            pltpu.VMEM((7, count, 8, B), F32),
            pltpu.VMEM((count, 8, B), F32),
            pltpu.VMEM((count, 64, B), F32),
            pltpu.VMEM((count, B, B), F32),
        ]

    outs = pl.pallas_call(
        kernel,
        out_shape=[square] * 5,
        in_specs=[smem] * 5 + [vmem] * 6,
        out_specs=[vmem] * 5,
        scratch_shapes=[
            pltpu.VMEM((3, 1024, B), F32),
            pltpu.VMEM((2, 64, 1024), F32),
            pltpu.VMEM((2, 8, 64, 1024), F32),
            pltpu.VMEM((2, 8, 64, 1024), BF16),
            pltpu.VMEM((2, 8, 64, 1024), BF16),
            pltpu.VMEM((4, 1024, B), BF16),
            pltpu.VMEM((4, 1024, B), BF16),
            pltpu.VMEM((4, 2, 2, B, B), F32),
            pltpu.VMEM((4, 2, B, B), F32),
            pltpu.VMEM((2, 2, 128, B), F32),
            pltpu.VMEM((2, 2, 128, B), F32),
            pltpu.VMEM((2, 2, 128, B), F32),
            pltpu.VMEM((2, 2, 128, B), F32),
            pltpu.VMEM((2, B, B), F32),
            pltpu.VMEM((2, B, B), F32),
            pltpu.VMEM((B, B), F32),
            pltpu.VMEM((B, B), F32),
            pltpu.VMEM((1, B, B), F32),
            pltpu.VMEM((8, B, B), F32),
            pltpu.VMEM((8, B, B), F32),
            pltpu.VMEM((B, B), F32),
            pltpu.VMEM((2, 4, 128, B), F32),
            pltpu.VMEM((2, 4, 128, B), F32),
            *chain(2),
            *chain(1),
            pltpu.SemaphoreType.DMA((SEMS,)),
            pltpu.SemaphoreType.DMA((SEMS,)),
        ],
        compiler_params=pltpu.CompilerParams(
            collective_id=0, has_side_effects=True, vmem_limit_bytes=56 * 1024 * 1024
        ),
    )(
        parent_one,
        widths_two,
        widths_one,
        pattern_two,
        pattern_one,
        inverse_anc,
        lower_two,
        lower_one,
        lower_par,
        dinv_two,
        dinv_one,
    )
    u2, g2, u1, pb, g1 = pl.pallas_call(
        settle,
        out_shape=[square, cube, square, cube, cube],
        in_specs=[vmem] * 5,
        out_specs=[vmem] * 5,
    )(outs[0], outs[2], outs[1], outs[3], outs[4])
    return u2, g2, u1, pb, g1


def solution(mesh):
    in_specs = (
        P("prow", "pcol"),
        P("prow", "pcol"),
        P(),
        P(),
        P("prow", None, None),
        P("prow", "pcol"),
        P(),
        P(),
        P(),
        P("prow", None, None),
        P("prow", None, None),
    )
    out_specs = (
        P("prow", "pcol"),
        P("prow", None, None),
        P("prow", "pcol"),
        P("prow", None, None),
        P("prow", None, None),
    )
    return jax.shard_map(
        per_device, mesh=mesh, in_specs=in_specs, out_specs=out_specs, check_vma=False
    )
```

```python
import functools

import jax
import jax.numpy as jnp
from jax import lax
from jax.experimental import pallas as pl
from jax.experimental.pallas import tpu as pltpu
from jax.sharding import PartitionSpec as P

B = 256
MESH = pl.DeviceIdType.MESH
F32 = jnp.float32
BF16 = jnp.bfloat16
NN = (((1,), (0,)), ((), ()))
NT = (((1,), (1,)), ((), ()))
SEMS = 300


def split(value):
    high = value.astype(BF16)
    return high, (value - high.astype(F32)).astype(BF16)


def dot3(lh, ll, rh, rl, dims=NN):
    dot = functools.partial(lax.dot_general, dimension_numbers=dims, preferred_element_type=F32)
    return dot(lh, rh) + (dot(lh, rl) + dot(ll, rh))


def mm(left, right, dims=NN):
    return dot3(*split(left), *split(right), dims)


def kernel(
    par, wid2, wid1, pat2, pat1, a, low2, low1, lpar, d2, d1,
    u2, u1, g2o, pbo, g1o,
    ag, lt, lg, lh, ll, ah, al, pp, rc, r_in, pl_in, f_in, s_out,
    lloc, lsnd, lpt, lpn, d2s, x2all, x2, x1, t_z, t_x, g_all,
    red_g, ry_g, yr_g, rz_g, zr_g, gz_g, fin_g,
    red_f, ry_f, yr_f, rz_f, zr_f, gz_f, fin_f,
    red_s, ry_s, yr_s, rz_s, zr_s, gz_s, fin_s,
    send_sem, recv_sem,
):
    r, q = lax.axis_index("prow"), lax.axis_index("pcol")
    k, c = lax.div(r, 2), lax.rem(r, 2)
    h, y, w = lax.div(q, 8), lax.rem(lax.div(q, 2), 4), lax.rem(q, 2)
    zi = 2 * k + w
    oc = 1 - c
    n = 2 * h + c

    def dev(k=k, c=c, h=h, y=y, w=w):
        return (2 * k + c, 8 * h + 2 * y + w)

    def ring(v, off, size=4):
        return lax.rem(v + (off + size), size)

    def zdev(v):
        return dev(k=lax.div(v, 2), w=lax.rem(v, 2))

    ids = [0]
    pending = []

    def take(count):
        ids[0] += count
        return ids[0] - count

    def copy(src, dst, device, recv=None, start=True):
        num = take(1)
        op = pltpu.make_async_remote_copy(
            src_ref=src,
            dst_ref=dst,
            send_sem=send_sem.at[num],
            recv_sem=recv_sem.at[num if recv is None else recv],
            device_id=device,
            device_id_type=MESH,
        )
        if start:
            op.start()
            pending.append(op)
        return op

    def arrival(dst, recv):
        return pltpu.make_async_remote_copy(
            src_ref=dst,
            dst_ref=dst,
            send_sem=send_sem.at[0],
            recv_sem=recv_sem.at[recv],
            device_id=dev(c=oc),
            device_id_type=MESH,
        )

    barrier = pltpu.get_barrier_semaphore()
    friends = [dev(c=oc)]
    friends += [dev(h=ring(h, o)) for o in (1, 2, 3)]
    friends += [dev(y=ring(y, o)) for o in (1, 2, 3)]
    friends += [zdev(ring(zi, o, 8)) for o in range(1, 8)]
    friends += [dev(h=ring(h, o), c=oc) for o in (1, 2, 3)]
    for friend in friends:
        pl.semaphore_signal(barrier, inc=1, device_id=friend, device_id_type=MESH)

    owner = lax.div(q, 4)
    inner = lax.rem(q, 4) * 64 + lax.broadcasted_iota(jnp.int32, (64, 1024), 0)
    block = lax.broadcasted_iota(jnp.int32, (64, 1024), 1) // B
    for lev, (low, pat, wid) in enumerate(((low2, pat2, wid2), (low1, pat1, wid1))):
        present = jnp.zeros((64, 1024), F32)
        for b in range(4):
            there = pat[owner, 4 * r + b].astype(F32)
            present = jnp.where(block == b, there, present)
        keep = jnp.where(inner < wid[owner], present, 0.0)
        lt[lev] = low[...] * keep
    row = lax.broadcasted_iota(jnp.int32, (B, B), 0)
    col = lax.broadcasted_iota(jnp.int32, (B, B), 1)
    inside = jnp.where(row < wid1[r], 1.0, 0.0) * jnp.where(col < wid2[par[r]], 1.0, 0.0)
    lpt[...] = lpar[0].T * inside

    pl.semaphore_wait(barrier, len(friends))

    hl, hr = dev(h=ring(h, -1)), dev(h=ring(h, 1))
    yl, yr = dev(y=ring(y, -1)), dev(y=ring(y, 1))
    sib, pair = dev(c=oc), dev(w=1 - w)
    mine = 2 * y + w
    theirs = 2 * y + 1 - w
    ml, mr, mf = 2 * ring(y, -1), 2 * ring(y, 1), 2 * ring(y, 2)
    top, bot = pl.ds(0, 512), pl.ds(512, 512)

    def split_l(lev, m):
        hi, lo = split(lg[lev, m])
        lh[lev, m] = hi
        ll[lev, m] = lo

    def send_own(lev):
        return (
            copy(lt.at[lev], lg.at[lev, mine], yr),
            copy(lt.at[lev], lg.at[lev, mine], yl),
        )

    def send_pair(lev):
        return (
            copy(lg.at[lev, theirs], lg.at[lev, theirs], yr),
            copy(lg.at[lev, theirs], lg.at[lev, theirs], yl),
        )

    def forward_l(lev, ops, which):
        near, far = pl.ds(0, 32), pl.ds(32, 32)
        ops[0].wait_recv()
        one = copy(lg.at[lev, ml + which, near], lg.at[lev, ml + which, near], yr)
        ops[1].wait_recv()
        two = copy(lg.at[lev, mr + which, far], lg.at[lev, mr + which, far], yl)
        return one, two

    def send_a(half):
        cols = pl.ds(128 * half, 128)
        return (
            copy(a.at[top, cols], ag.at[0, half, top], hr),
            copy(a.at[bot, cols], ag.at[1, half, bot], hl),
            copy(a.at[bot, cols], ag.at[0, half, bot], hr),
            copy(a.at[top, cols], ag.at[1, half, top], hl),
        )

    def forward_a(half, ops):
        ops[0].wait_recv()
        one = copy(ag.at[0, half, top], ag.at[2, half, top], hr)
        ops[1].wait_recv()
        two = copy(ag.at[1, half, bot], ag.at[2, half, bot], hl)
        return one, two

    def split_a(half, rel):
        hi, lo = split(a[:, 128 * half : 128 * half + 128] if rel == 0 else ag[rel - 1, half])
        cols = slice(128 * (rel % 2), 128 * (rel % 2) + 128)
        ah[half, rel // 2, :, cols] = hi
        al[half, rel // 2, :, cols] = lo

    w2 = copy(lt.at[0], lg.at[0, mine], pair)
    o2 = send_own(0)
    a0 = send_a(0)
    d2c = copy(d2, d2s, sib)

    rows32 = pl.ds(pl.multiple_of(mine * 32, 32), 32)
    rows64 = pl.ds(pl.multiple_of(y * 64, 64), 64)
    lp_recv = ids[0]
    lp_ops = [
        copy(lpt.at[rows32], lpn.at[rows32], dev(k=ring(k, o)), recv=lp_recv, start=False)
        for o in (1, 2, 3)
    ]

    @pl.when(h == k)
    def _():
        lpn[rows32] = lpt[rows32]
        for op in lp_ops:
            op.start()

    lg[0, mine] = lt[0]
    lg[1, mine] = lt[1]
    split_l(0, mine)
    split_l(1, mine)
    split_a(0, 0)
    split_a(1, 0)
    w2.wait_recv()
    p2 = send_pair(0)
    f2 = forward_l(0, o2, w)
    split_l(0, theirs)
    split_l(0, ml + w)
    split_l(0, mr + w)
    fa0 = forward_a(0, a0)
    a1 = send_a(1)
    w1 = copy(lt.at[1], lg.at[1, mine], pair)
    e2 = forward_l(0, p2, 1 - w)
    o1 = send_own(1)
    split_l(0, ml + 1 - w)
    split_l(0, mr + 1 - w)
    a0[2].wait_recv()
    split_a(0, 1)
    a0[3].wait_recv()
    split_a(0, 2)
    for op in f2:
        op.wait_recv()
    split_l(0, mf + w)
    for op in e2:
        op.wait_recv()
    split_l(0, mf + 1 - w)

    cy = lax.div(y, 2)
    off = pl.multiple_of(lax.rem(mine, 4) * B, B)
    l_ops = [copy(lsnd.at[lev], lloc.at[lev], sib, start=False) for lev in range(2)]

    def share(lev):
        @pl.when(c == cy)
        def _():
            lsnd[lev] = lg[lev, pl.ds(4 * oc, 4), :, pl.ds(off, B)].reshape(B, B)
            l_ops[lev].start()
            lloc[lev] = lg[lev, pl.ds(4 * c, 4), :, pl.ds(off, B)].reshape(B, B)

        @pl.when(c != cy)
        def _():
            l_ops[lev].wait_recv()

    kp, km, ko = ring(k, 1), ring(k, -1), ring(k, 2)
    zp, zm = dev(k=kp), dev(k=km)
    up, dn = pl.ds(0, 128), pl.ds(128, 128)
    slots = (h, ring(h, -1), ring(h, 1), ring(h, 2))

    def product(lev, half, duo):
        def part(parity):
            left_h = lh[lev, pl.ds(4 * parity, 4)].reshape(B, 1024)
            left_l = ll[lev, pl.ds(4 * parity, 4)].reshape(B, 1024)
            value = dot3(left_h, left_l, ah[half, duo], al[half, duo])
            for side in range(2):
                pp[lev, half, slots[2 * duo + side], parity] = value[:, 128 * side : 128 * side + 128]

        part(oc)
        ops = []
        for side in range(2):
            slot = slots[2 * duo + side]
            ops.append(copy(pp.at[lev, half, slot, oc], rc.at[lev, half, slot], sib))
        part(c)
        return [(lev, half, slots[2 * duo + side], ops[side]) for side in range(2)]

    def add_cores(parts):
        for lev, half, slot, op in parts:
            op.wait_recv()
            pp[lev, half, slot, c] += rc[lev, half, slot]

    def reduce_start(lev, half):
        mine_of = pp.at[lev, half]
        return [
            copy(mine_of.at[ko, c, up], r_in.at[lev, half, 0], zp),
            copy(mine_of.at[ko, c, dn], r_in.at[lev, half, 1], zm),
            copy(mine_of.at[kp, c, dn], pl_in.at[lev, half, 0], zp),
            copy(mine_of.at[km, c, up], pl_in.at[lev, half, 1], zm),
        ]

    def relay(lev, half, ops):
        ops[0].wait_recv()
        s_out[lev, half, 0] = r_in[lev, half, 0] + pp[lev, half, kp, c, up]
        ops.append(copy(s_out.at[lev, half, 0], f_in.at[lev, half, 0], zp))
        ops[1].wait_recv()
        s_out[lev, half, 1] = r_in[lev, half, 1] + pp[lev, half, km, c, dn]
        ops.append(copy(s_out.at[lev, half, 1], f_in.at[lev, half, 1], zm))

    def total(lev, half, ops):
        for op in ops[2:]:
            op.wait_recv()
        upper = pp[lev, half, k, c, up] + f_in[lev, half, 0] + pl_in[lev, half, 1]
        lower = pp[lev, half, k, c, dn] + f_in[lev, half, 1] + pl_in[lev, half, 0]
        return jnp.concatenate([upper, lower], axis=0)

    class Place:
        def __init__(self, piece, buf, out):
            tz, tx = t_z.at[piece], t_x.at[piece]
            self.buf, self.out, self.tz, self.tx = buf, out, tz, tx
            self.z_base, self.x_base = take(4), take(4)
            self.got_z, self.got_x = take(1), take(1)
            self.via_z = copy(
                buf.at[up], tz.at[k], dev(k=h), recv=self.z_base + ring(k, 4 - h), start=False
            )
            self.via_x = copy(
                buf.at[dn], tx.at[h], dev(h=k), recv=self.x_base + ring(h, 4 - k), start=False
            )
            self.on_z, self.on_x = [], []
            for o in (1, 2, 3):
                v = ring(k, o)
                self.on_z.append(
                    copy(tz.at[v], out.at[up], dev(h=v), recv=self.got_z, start=False)
                )
                self.on_x.append(
                    copy(tx.at[v], out.at[dn], dev(k=v), recv=self.got_x, start=False)
                )

        def begin_x(self):
            @pl.when(h != k)
            def _():
                self.via_x.start()

            @pl.when(h == k)
            def _():
                self.out[...] = self.buf[...]

        def begin_z(self):
            @pl.when(h != k)
            def _():
                self.via_z.start()

        def pass_x(self):
            @pl.when(h == k)
            def _():
                for o in (1, 2, 3):
                    arrival(self.tx.at[ring(k, o)], self.x_base + o).wait_recv()
                    self.on_x[o - 1].start()

        def pass_z(self):
            @pl.when(h == k)
            def _():
                for o in (1, 2, 3):
                    arrival(self.tz.at[ring(k, o)], self.z_base + o).wait_recv()
                    self.on_z[o - 1].start()

        def finish(self):
            @pl.when(h != k)
            def _():
                self.via_z.wait_send()
                self.via_x.wait_send()
                arrival(self.out.at[up], self.got_z).wait_recv()
                arrival(self.out.at[dn], self.got_x).wait_recv()

            @pl.when(h == k)
            def _():
                for op in self.on_z + self.on_x:
                    op.wait_send()

    left, right = pl.ds(0, 128), pl.ds(128, 128)
    place_20 = Place(0, x2.at[:, left], u2.at[:, left])
    place_21 = Place(1, x2.at[:, right], u2.at[:, right])
    place_10 = Place(2, x1.at[:, left], u1.at[:, left])
    place_11 = Place(3, x1.at[:, right], u1.at[:, right])

    def x2_half(half, ops):
        value = -total(0, half, ops)
        x2[:, 128 * half : 128 * half + 128] = value
        x2all[half, n] = value

    duo = product(0, 0, 0)
    for op in fa0:
        op.wait_recv()
    split_a(0, 3)
    add_cores(duo + product(0, 0, 1))
    rs00 = reduce_start(0, 0)
    share(0)
    w1.wait_recv()
    p1 = send_pair(1)
    f1 = forward_l(1, o1, w)
    split_l(1, theirs)
    split_l(1, ml + w)
    split_l(1, mr + w)
    fa1 = forward_a(1, a1)
    relay(0, 0, rs00)
    e1 = forward_l(1, p1, 1 - w)

    @pl.when(h != k)
    def _():
        lp_ops[0].wait_recv()

    lp_w = copy(lpn.at[rows32], lpn.at[rows32], pair)
    split_l(1, ml + 1 - w)
    split_l(1, mr + 1 - w)
    a1[2].wait_recv()
    split_a(1, 1)
    a1[3].wait_recv()
    split_a(1, 2)
    duo = product(0, 1, 0)
    for op in f1:
        op.wait_recv()
    split_l(1, mf + w)
    x2_half(0, rs00)
    place_20.begin_x()
    place_20.begin_z()
    for op in fa1:
        op.wait_recv()
    split_a(1, 3)
    add_cores(duo + product(0, 1, 1))
    rs01 = reduce_start(0, 1)
    for op in e1:
        op.wait_recv()
    split_l(1, mf + 1 - w)

    def gather_start(buf):
        return copy(buf.at[n], buf.at[n], hr), copy(buf.at[n], buf.at[n], hl), copy(
            buf.at[n], buf.at[n], sib
        )

    def gather_mid(buf, ops):
        left, right = 2 * ring(h, -1) + c, 2 * ring(h, 1) + c
        ops[0].wait_recv()
        one = copy(buf.at[left, up], buf.at[left, up], hr)
        sib_l = copy(buf.at[left], buf.at[left], sib)
        ops[1].wait_recv()
        two = copy(buf.at[right, dn], buf.at[right, dn], hl)
        sib_r = copy(buf.at[right], buf.at[right], sib)
        return one, two, ops[2], sib_l, sib_r

    def gather_end(buf, ops):
        opp = 2 * ring(h, 2) + c
        ops[0].wait_recv()
        ops[1].wait_recv()
        last = copy(buf.at[opp], buf.at[opp], sib)
        for op in ops[2:]:
            op.wait_recv()
        last.wait_recv()

    x20 = gather_start(x2all.at[0])
    lp_w.wait_recv()
    lp_y = [copy(lpn.at[rows64], lpn.at[rows64], dev(y=ring(y, o))) for o in (1, 2, 3)]
    duo = product(1, 0, 0)
    add_cores(duo + product(1, 0, 1))
    rs10 = reduce_start(1, 0)
    relay(0, 1, rs01)
    duo = product(1, 1, 0)
    add_cores(duo + product(1, 1, 1))
    rs11 = reduce_start(1, 1)
    share(1)
    place_20.pass_x()
    place_20.pass_z()
    x20 = gather_mid(x2all.at[0], x20)
    relay(1, 0, rs10)

    own8 = pl.ds(pl.multiple_of(zi * 8, 8), 8)

    class Chain:
        def __init__(self, red, ry, yr, rz, zr, gz, fin):
            self.bufs = (red, ry, yr, rz, zr, gz, fin)

        def y_start(self):
            red, ry = self.bufs[:2]
            self.ops = []
            for o in (1, 2, 3):
                to = ring(y, o)
                part = pl.ds(pl.multiple_of(to * 64, 64), 64)
                self.ops.append(copy(red.at[:, part], ry.at[o - 1], dev(y=to)))

        def z_start(self):
            red, ry, yr, rz = self.bufs[:4]
            acc = red[:, rows64, :]
            for o in range(3):
                self.ops[o].wait_recv()
                acc = acc + ry[o]
            yr[...] = acc
            self.ops = []
            for o in range(1, 8):
                to = ring(zi, o, 8)
                part = pl.ds(pl.multiple_of(to * 8, 8), 8)
                self.ops.append(copy(yr.at[:, part], rz.at[o - 1], zdev(to)))

        def plane_start(self, less=None):
            yr, rz, zr, gz = self.bufs[2:6]
            acc = yr[:, own8, :]
            for o in range(7):
                self.ops[o].wait_recv()
                acc = acc + rz[o]
            zr[...] = acc if less is None else acc - less[None]
            self.base = take(8)
            self.sends = []
            for v in (0, 1):
                op = copy(
                    zr, gz.at[:, own8], dev(k=h, w=v), recv=self.base + zi, start=False
                )
                self.sends.append(op)

                @pl.when(2 * h + v != zi)
                def _(op=op):
                    op.start()

        def x_send(self):
            zr, gz = self.bufs[4:6]
            got = ids[0]
            self.spread = [
                copy(gz, gz, dev(h=ring(h, o)), recv=got, start=False) for o in (1, 2, 3)
            ]

            @pl.when(h == k)
            def _():
                gz[:, own8, :] = zr[...]
                for o in range(1, 8):
                    frm = ring(zi, o, 8)
                    part = pl.ds(pl.multiple_of(frm * 8, 8), 8)
                    arrival(gz.at[:, part], self.base + frm).wait_recv()
                for op in self.spread:
                    op.start()

        def x_recv(self):
            @pl.when(h != k)
            def _():
                self.spread[0].wait_recv()

        def y_spread(self):
            gz, fin = self.bufs[5:]
            self.ops = [copy(gz, fin.at[:, rows64], dev(y=ring(y, o))) for o in (1, 2, 3)]
            fin[:, rows64, :] = gz[...]

        def finish(self):
            for op in self.ops:
                op.wait_recv()

        def drain(self):
            for v in (0, 1):

                @pl.when(2 * h + v != zi)
                def _(v=v):
                    self.sends[v].wait_send()

            @pl.when(h == k)
            def _():
                for op in self.spread:
                    op.wait_send()

    sum_g = Chain(red_g, ry_g, yr_g, rz_g, zr_g, gz_g, fin_g)
    sum_f = Chain(red_f, ry_f, yr_f, rz_f, zr_f, gz_f, fin_f)
    sum_s = Chain(red_s, ry_s, yr_s, rz_s, zr_s, gz_s, fin_s)
    x2_half(1, rs01)
    place_21.begin_x()
    x21 = gather_start(x2all.at[1])
    red_g[0] = mm(lloc[0], x2[...], NT)
    sum_g.y_start()
    gather_end(x2all.at[0], x20)
    relay(1, 1, rs11)
    for op in lp_y:
        op.wait_recv()
    parent = par[n]
    lp_h, lp_l = split(lpn[...])
    d2c.wait_recv()
    here = jnp.where(parent == r, 1.0, 0.0)
    beside = jnp.where(parent == 2 * k + oc, 1.0, 0.0)
    own_rows = dot3(*split(d2[0, rows32] * here + d2s[0, rows32] * beside), lp_h, lp_l, NT)
    sum_g.z_start()
    x21 = gather_mid(x2all.at[1], x21)
    sum_g.plane_start()
    g_all[n] = zr_g[0]
    slices = [copy(g_all.at[n], g_all.at[n], sib)]
    for o in (1, 2, 3):
        for core in (c, oc):
            slices.append(copy(g_all.at[n], g_all.at[n], dev(h=ring(h, o), c=core)))
    gather_end(x2all.at[1], x21)
    x2p = jnp.concatenate([x2all[0, parent], x2all[1, parent]], axis=1)
    red_f[0] = mm(x2p, lloc[1], NT)
    red_f[0, rows32] += own_rows
    sum_f.y_start()
    correction = dot3(lp_h, lp_l, *split(x2p))
    sum_g.x_send()
    x1[:, 0:128] = -total(1, 0, rs10) - correction[:, 0:128]
    x1[:, 128:256] = -total(1, 1, rs11) - correction[:, 128:256]
    place_10.begin_x()
    place_11.begin_x()
    red_s[0] = mm(lloc[1], x1[...], NT)
    sum_s.y_start()
    sum_f.z_start()
    sum_g.x_recv()
    sum_g.y_spread()
    sum_s.z_start()
    for op in slices:
        op.wait_recv()
    sum_f.plane_start(dot3(*split(g_all[parent]), lp_h, lp_l, NT))
    sum_s.plane_start()
    later = (place_21, place_10, place_11)
    for move in later:
        move.begin_z()
        move.pass_x()
    sum_f.x_send()
    sum_s.x_send()
    sum_f.x_recv()
    sum_f.y_spread()
    sum_g.finish()
    g2o[...] = d2[0] - fin_g[0]
    sum_s.x_recv()
    sum_s.y_spread()
    for move in later:
        move.pass_z()
    sum_f.finish()
    pb = -fin_f[0]
    pbo[...] = pb
    update = d1[0] - mm(lpt[...], pb)
    sum_s.finish()
    g1o[...] = update - fin_s[0]
    place_20.finish()
    for move in later:
        move.finish()

    for chain in (sum_g, sum_f, sum_s):
        chain.drain()

    @pl.when(h == k)
    def _():
        for op in lp_ops:
            op.wait_send()

    @pl.when(c == cy)
    def _():
        for op in l_ops:
            op.wait_send()

    for op in pending:
        op.wait_send()
    assert ids[0] <= SEMS


def settle(*refs):
    for src, dst in zip(refs[:5], refs[5:]):
        dst[...] = src[...].reshape(dst.shape)


def per_device(
    inverse_anc,
    lower_two,
    pattern_two,
    widths_two,
    dinv_two,
    lower_one,
    pattern_one,
    widths_one,
    parent_one,
    lower_par,
    dinv_one,
):
    vmem = pl.BlockSpec(memory_space=pltpu.VMEM)
    smem = pl.BlockSpec(memory_space=pltpu.SMEM)
    square = jax.ShapeDtypeStruct((B, B), F32)
    cube = jax.ShapeDtypeStruct((1, B, B), F32)

    def chain(count):
        return [
            pltpu.VMEM((count, B, B), F32),
            pltpu.VMEM((3, count, 64, B), F32),
            pltpu.VMEM((count, 64, B), F32),
            pltpu.VMEM((7, count, 8, B), F32),
            pltpu.VMEM((count, 8, B), F32),
            pltpu.VMEM((count, 64, B), F32),
            pltpu.VMEM((count, B, B), F32),
        ]

    outs = pl.pallas_call(
        kernel,
        out_shape=[square] * 5,
        in_specs=[smem] * 5 + [vmem] * 6,
        out_specs=[vmem] * 5,
        scratch_shapes=[
            pltpu.VMEM((3, 2, 1024, 128), F32),
            pltpu.VMEM((2, 64, 1024), F32),
            pltpu.VMEM((2, 8, 64, 1024), F32),
            pltpu.VMEM((2, 8, 64, 1024), BF16),
            pltpu.VMEM((2, 8, 64, 1024), BF16),
            pltpu.VMEM((2, 2, 1024, B), BF16),
            pltpu.VMEM((2, 2, 1024, B), BF16),
            pltpu.VMEM((2, 2, 4, 2, B, 128), F32),
            pltpu.VMEM((2, 2, 4, B, 128), F32),
            pltpu.VMEM((2, 2, 2, 128, 128), F32),
            pltpu.VMEM((2, 2, 2, 128, 128), F32),
            pltpu.VMEM((2, 2, 2, 128, 128), F32),
            pltpu.VMEM((2, 2, 2, 128, 128), F32),
            pltpu.VMEM((2, B, B), F32),
            pltpu.VMEM((2, B, B), F32),
            pltpu.VMEM((B, B), F32),
            pltpu.VMEM((B, B), F32),
            pltpu.VMEM((1, B, B), F32),
            pltpu.VMEM((2, 8, B, 128), F32),
            pltpu.VMEM((B, B), F32),
            pltpu.VMEM((B, B), F32),
            pltpu.VMEM((4, 4, 128, 128), F32),
            pltpu.VMEM((4, 4, 128, 128), F32),
            pltpu.VMEM((8, 8, B), F32),
            *chain(1),
            *chain(1),
            *chain(1),
            pltpu.SemaphoreType.DMA((SEMS,)),
            pltpu.SemaphoreType.DMA((SEMS,)),
        ],
        compiler_params=pltpu.CompilerParams(
            collective_id=0, has_side_effects=True, vmem_limit_bytes=56 * 1024 * 1024
        ),
    )(
        parent_one,
        widths_two,
        widths_one,
        pattern_two.T,
        pattern_one.T,
        inverse_anc,
        lower_two.T,
        lower_one.T,
        lower_par,
        dinv_two,
        dinv_one,
    )
    u2, g2, u1, pb, g1 = pl.pallas_call(
        settle,
        out_shape=[square, cube, square, cube, cube],
        in_specs=[vmem] * 5,
        out_specs=[vmem] * 5,
    )(outs[0], outs[2], outs[1], outs[3], outs[4])
    return u2, g2, u1, pb, g1


def solution(mesh):
    in_specs = (
        P("prow", "pcol"),
        P("prow", "pcol"),
        P(),
        P(),
        P("prow", None, None),
        P("prow", "pcol"),
        P(),
        P(),
        P(),
        P("prow", None, None),
        P("prow", None, None),
    )
    out_specs = (
        P("prow", "pcol"),
        P("prow", None, None),
        P("prow", "pcol"),
        P("prow", None, None),
        P("prow", None, None),
    )
    return jax.shard_map(
        per_device, mesh=mesh, in_specs=in_specs, out_specs=out_specs, check_vma=False
    )
```

```python
import functools

import jax
import jax.numpy as jnp
from jax import lax
from jax.experimental import pallas as pl
from jax.experimental.pallas import tpu as pltpu
from jax.sharding import PartitionSpec as P

B = 256
MESH = pl.DeviceIdType.MESH
F32 = jnp.float32
BF16 = jnp.bfloat16
NN = (((1,), (0,)), ((), ()))
NT = (((1,), (1,)), ((), ()))
SEMS = 300


def split(value):
    high = value.astype(BF16)
    return high, (value - high.astype(F32)).astype(BF16)


def dot3(lh, ll, rh, rl, dims=NN):
    dot = functools.partial(lax.dot_general, dimension_numbers=dims, preferred_element_type=F32)
    return dot(lh, rh) + (dot(lh, rl) + dot(ll, rh))


def mm(left, right, dims=NN):
    return dot3(*split(left), *split(right), dims)


def kernel(
    par, wid2, wid1, pat2, pat1, a, low2, low1, lpar, d2, d1,
    u2, u1, g2o, pbo, g1o,
    ag, lt, lg, lh, ll, ah, al, pp, rc, r_in, pl_in, f_in, s_out,
    lloc, lsnd, lpt, lpn, d2s, x2all, x2, x1, t_z, t_x, g_all,
    red_g, ry_g, yr_g, rz_g, zr_g, gz_g, fin_g,
    red_f, ry_f, yr_f, rz_f, zr_f, gz_f, fin_f,
    red_s, ry_s, yr_s, rz_s, zr_s, gz_s, fin_s,
    send_sem, recv_sem,
):
    r, q = lax.axis_index("prow"), lax.axis_index("pcol")
    k, c = lax.div(r, 2), lax.rem(r, 2)
    h, y, w = lax.div(q, 8), lax.rem(lax.div(q, 2), 4), lax.rem(q, 2)
    zi = 2 * k + w
    oc = 1 - c
    n = 2 * h + c

    def dev(k=k, c=c, h=h, y=y, w=w):
        return (2 * k + c, 8 * h + 2 * y + w)

    def ring(v, off, size=4):
        return lax.rem(v + (off + size), size)

    def zdev(v):
        return dev(k=lax.div(v, 2), w=lax.rem(v, 2))

    ids = [0]
    pending = []

    def take(count):
        ids[0] += count
        return ids[0] - count

    def copy(src, dst, device, recv=None, start=True):
        num = take(1)
        op = pltpu.make_async_remote_copy(
            src_ref=src,
            dst_ref=dst,
            send_sem=send_sem.at[num],
            recv_sem=recv_sem.at[num if recv is None else recv],
            device_id=device,
            device_id_type=MESH,
        )
        if start:
            op.start()
            pending.append(op)
        return op

    def arrival(dst, recv):
        return pltpu.make_async_remote_copy(
            src_ref=dst,
            dst_ref=dst,
            send_sem=send_sem.at[0],
            recv_sem=recv_sem.at[recv],
            device_id=dev(c=oc),
            device_id_type=MESH,
        )

    barrier = pltpu.get_barrier_semaphore()
    friends = [dev(c=oc)]
    friends += [dev(h=ring(h, o)) for o in (1, 2, 3)]
    friends += [dev(y=ring(y, o)) for o in (1, 2, 3)]
    friends += [zdev(ring(zi, o, 8)) for o in range(1, 8)]
    friends += [dev(h=ring(h, o), c=oc) for o in (1, 2, 3)]
    for friend in friends:
        pl.semaphore_signal(barrier, inc=1, device_id=friend, device_id_type=MESH)

    owner = lax.div(q, 4)
    inner = lax.rem(q, 4) * 64 + lax.broadcasted_iota(jnp.int32, (64, 1024), 0)
    block = lax.broadcasted_iota(jnp.int32, (64, 1024), 1) // B
    for lev, (low, pat, wid) in enumerate(((low2, pat2, wid2), (low1, pat1, wid1))):
        present = jnp.zeros((64, 1024), F32)
        for b in range(4):
            there = pat[owner, 4 * r + b].astype(F32)
            present = jnp.where(block == b, there, present)
        keep = jnp.where(inner < wid[owner], present, 0.0)
        lt[lev] = low[...] * keep
    row = lax.broadcasted_iota(jnp.int32, (B, B), 0)
    col = lax.broadcasted_iota(jnp.int32, (B, B), 1)
    inside = jnp.where(row < wid1[r], 1.0, 0.0) * jnp.where(col < wid2[par[r]], 1.0, 0.0)
    lpt[...] = lpar[0].T * inside

    pl.semaphore_wait(barrier, len(friends))

    hl, hr = dev(h=ring(h, -1)), dev(h=ring(h, 1))
    yl, yr = dev(y=ring(y, -1)), dev(y=ring(y, 1))
    sib, pair = dev(c=oc), dev(w=1 - w)
    mine = 2 * y + w
    theirs = 2 * y + 1 - w
    ml, mr, mf = 2 * ring(y, -1), 2 * ring(y, 1), 2 * ring(y, 2)
    top, bot = pl.ds(0, 512), pl.ds(512, 512)

    def split_l(lev, m):
        hi, lo = split(lg[lev, m])
        lh[lev, m] = hi
        ll[lev, m] = lo

    def send_own(lev):
        return (
            copy(lt.at[lev], lg.at[lev, mine], yr),
            copy(lt.at[lev], lg.at[lev, mine], yl),
        )

    def send_pair(lev):
        return (
            copy(lg.at[lev, theirs], lg.at[lev, theirs], yr),
            copy(lg.at[lev, theirs], lg.at[lev, theirs], yl),
        )

    def forward_l(lev, ops, which):
        near, far = pl.ds(0, 32), pl.ds(32, 32)
        ops[0].wait_recv()
        one = copy(lg.at[lev, ml + which, near], lg.at[lev, ml + which, near], yr)
        ops[1].wait_recv()
        two = copy(lg.at[lev, mr + which, far], lg.at[lev, mr + which, far], yl)
        return one, two

    def send_a(half):
        cols = pl.ds(128 * half, 128)
        return (
            copy(a.at[top, cols], ag.at[0, half, top], hr),
            copy(a.at[bot, cols], ag.at[1, half, bot], hl),
            copy(a.at[bot, cols], ag.at[0, half, bot], hr),
            copy(a.at[top, cols], ag.at[1, half, top], hl),
        )

    def forward_a(half, ops):
        ops[0].wait_recv()
        one = copy(ag.at[0, half, top], ag.at[2, half, top], hr)
        ops[1].wait_recv()
        two = copy(ag.at[1, half, bot], ag.at[2, half, bot], hl)
        return one, two

    def split_a(half, rel):
        hi, lo = split(a[:, 128 * half : 128 * half + 128] if rel == 0 else ag[rel - 1, half])
        cols = slice(128 * (rel % 2), 128 * (rel % 2) + 128)
        ah[half, rel // 2, :, cols] = hi
        al[half, rel // 2, :, cols] = lo

    w2 = copy(lt.at[0], lg.at[0, mine], pair)
    o2 = send_own(0)
    a0 = send_a(0)
    d2c = copy(d2, d2s, sib)

    rows32 = pl.ds(pl.multiple_of(mine * 32, 32), 32)
    rows64 = pl.ds(pl.multiple_of(y * 64, 64), 64)
    lp_recv = ids[0]
    lp_ops = [
        copy(lpt.at[rows32], lpn.at[rows32], dev(k=ring(k, o)), recv=lp_recv, start=False)
        for o in (1, 2, 3)
    ]

    @pl.when(h == k)
    def _():
        lpn[rows32] = lpt[rows32]
        for op in lp_ops:
            op.start()

    lg[0, mine] = lt[0]
    lg[1, mine] = lt[1]
    split_l(0, mine)
    split_l(1, mine)
    split_a(0, 0)
    split_a(1, 0)
    w2.wait_recv()
    p2 = send_pair(0)
    f2 = forward_l(0, o2, w)
    split_l(0, theirs)
    split_l(0, ml + w)
    split_l(0, mr + w)
    fa0 = forward_a(0, a0)
    a1 = send_a(1)
    w1 = copy(lt.at[1], lg.at[1, mine], pair)
    e2 = forward_l(0, p2, 1 - w)
    o1 = send_own(1)
    split_l(0, ml + 1 - w)
    split_l(0, mr + 1 - w)
    a0[2].wait_recv()
    split_a(0, 1)
    a0[3].wait_recv()
    split_a(0, 2)
    for op in f2:
        op.wait_recv()
    split_l(0, mf + w)
    for op in e2:
        op.wait_recv()
    split_l(0, mf + 1 - w)

    cy = lax.div(y, 2)
    off = pl.multiple_of(lax.rem(mine, 4) * B, B)
    l_ops = [copy(lsnd.at[lev], lloc.at[lev], sib, start=False) for lev in range(2)]

    def share(lev):
        @pl.when(c == cy)
        def _():
            lsnd[lev] = lg[lev, pl.ds(4 * oc, 4), :, pl.ds(off, B)].reshape(B, B)
            l_ops[lev].start()
            lloc[lev] = lg[lev, pl.ds(4 * c, 4), :, pl.ds(off, B)].reshape(B, B)

        @pl.when(c != cy)
        def _():
            l_ops[lev].wait_recv()

    kp, km, ko = ring(k, 1), ring(k, -1), ring(k, 2)
    zp, zm = dev(k=kp), dev(k=km)
    up, dn = pl.ds(0, 128), pl.ds(128, 128)
    slots = (h, ring(h, -1), ring(h, 1), ring(h, 2))

    def product(lev, half, duo):
        def part(parity):
            left_h = lh[lev, pl.ds(4 * parity, 4)].reshape(B, 1024)
            left_l = ll[lev, pl.ds(4 * parity, 4)].reshape(B, 1024)
            value = dot3(left_h, left_l, ah[half, duo], al[half, duo])
            for side in range(2):
                pp[lev, half, slots[2 * duo + side], parity] = value[:, 128 * side : 128 * side + 128]

        part(oc)
        ops = []
        for side in range(2):
            slot = slots[2 * duo + side]
            ops.append(copy(pp.at[lev, half, slot, oc], rc.at[lev, half, slot], sib))
        part(c)
        return [(lev, half, slots[2 * duo + side], ops[side]) for side in range(2)]

    def add_cores(parts):
        for lev, half, slot, op in parts:
            op.wait_recv()
            pp[lev, half, slot, c] += rc[lev, half, slot]

    def reduce_start(lev, half):
        mine_of = pp.at[lev, half]
        return [
            copy(mine_of.at[ko, c, up], r_in.at[lev, half, 0], zp),
            copy(mine_of.at[ko, c, dn], r_in.at[lev, half, 1], zm),
            copy(mine_of.at[kp, c, dn], pl_in.at[lev, half, 0], zp),
            copy(mine_of.at[km, c, up], pl_in.at[lev, half, 1], zm),
        ]

    def relay(lev, half, ops):
        ops[0].wait_recv()
        s_out[lev, half, 0] = r_in[lev, half, 0] + pp[lev, half, kp, c, up]
        ops.append(copy(s_out.at[lev, half, 0], f_in.at[lev, half, 0], zp))
        ops[1].wait_recv()
        s_out[lev, half, 1] = r_in[lev, half, 1] + pp[lev, half, km, c, dn]
        ops.append(copy(s_out.at[lev, half, 1], f_in.at[lev, half, 1], zm))

    def total(lev, half, ops):
        for op in ops[2:]:
            op.wait_recv()
        upper = pp[lev, half, k, c, up] + f_in[lev, half, 0] + pl_in[lev, half, 1]
        lower = pp[lev, half, k, c, dn] + f_in[lev, half, 1] + pl_in[lev, half, 0]
        return jnp.concatenate([upper, lower], axis=0)

    class Place:
        def __init__(self, piece, buf, out):
            tz, tx = t_z.at[piece], t_x.at[piece]
            self.buf, self.out, self.tz, self.tx = buf, out, tz, tx
            self.z_base, self.x_base = take(4), take(4)
            self.got_z, self.got_x = take(1), take(1)
            self.via_z = copy(
                buf.at[up], tz.at[k], dev(k=h), recv=self.z_base + ring(k, 4 - h), start=False
            )
            self.via_x = copy(
                buf.at[dn], tx.at[h], dev(h=k), recv=self.x_base + ring(h, 4 - k), start=False
            )
            self.on_z, self.on_x = [], []
            for o in (1, 2, 3):
                v = ring(k, o)
                self.on_z.append(
                    copy(tz.at[v], out.at[up], dev(h=v), recv=self.got_z, start=False)
                )
                self.on_x.append(
                    copy(tx.at[v], out.at[dn], dev(k=v), recv=self.got_x, start=False)
                )

        def begin_x(self):
            @pl.when(h != k)
            def _():
                self.via_x.start()

            @pl.when(h == k)
            def _():
                self.out[...] = self.buf[...]

        def begin_z(self):
            @pl.when(h != k)
            def _():
                self.via_z.start()

        def pass_x(self):
            @pl.when(h == k)
            def _():
                for o in (1, 2, 3):
                    arrival(self.tx.at[ring(k, o)], self.x_base + o).wait_recv()
                    self.on_x[o - 1].start()

        def pass_z(self):
            @pl.when(h == k)
            def _():
                for o in (1, 2, 3):
                    arrival(self.tz.at[ring(k, o)], self.z_base + o).wait_recv()
                    self.on_z[o - 1].start()

        def finish(self):
            @pl.when(h != k)
            def _():
                self.via_z.wait_send()
                self.via_x.wait_send()
                arrival(self.out.at[up], self.got_z).wait_recv()
                arrival(self.out.at[dn], self.got_x).wait_recv()

            @pl.when(h == k)
            def _():
                for op in self.on_z + self.on_x:
                    op.wait_send()

    left, right = pl.ds(0, 128), pl.ds(128, 128)
    place_20 = Place(0, x2.at[:, left], u2.at[:, left])
    place_21 = Place(1, x2.at[:, right], u2.at[:, right])
    place_10 = Place(2, x1.at[:, left], u1.at[:, left])
    place_11 = Place(3, x1.at[:, right], u1.at[:, right])

    def x2_half(half, ops):
        value = -total(0, half, ops)
        x2[:, 128 * half : 128 * half + 128] = value
        x2all[half, n] = value

    duo = product(0, 0, 0)
    for op in fa0:
        op.wait_recv()
    split_a(0, 3)
    add_cores(duo + product(0, 0, 1))
    rs00 = reduce_start(0, 0)
    share(0)
    w1.wait_recv()
    p1 = send_pair(1)
    f1 = forward_l(1, o1, w)
    split_l(1, theirs)
    split_l(1, ml + w)
    split_l(1, mr + w)
    fa1 = forward_a(1, a1)
    relay(0, 0, rs00)
    e1 = forward_l(1, p1, 1 - w)

    @pl.when(h != k)
    def _():
        lp_ops[0].wait_recv()

    lp_w = copy(lpn.at[rows32], lpn.at[rows32], pair)
    split_l(1, ml + 1 - w)
    split_l(1, mr + 1 - w)
    a1[2].wait_recv()
    split_a(1, 1)
    a1[3].wait_recv()
    split_a(1, 2)
    duo = product(0, 1, 0)
    for op in f1:
        op.wait_recv()
    split_l(1, mf + w)
    x2_half(0, rs00)
    place_20.begin_x()
    place_20.begin_z()
    for op in fa1:
        op.wait_recv()
    split_a(1, 3)
    add_cores(duo + product(0, 1, 1))
    rs01 = reduce_start(0, 1)
    for op in e1:
        op.wait_recv()
    split_l(1, mf + 1 - w)

    def gather_start(buf):
        return copy(buf.at[n], buf.at[n], hr), copy(buf.at[n], buf.at[n], hl), copy(
            buf.at[n], buf.at[n], sib
        )

    def gather_mid(buf, ops):
        left, right = 2 * ring(h, -1) + c, 2 * ring(h, 1) + c
        ops[0].wait_recv()
        one = copy(buf.at[left, up], buf.at[left, up], hr)
        sib_l = copy(buf.at[left], buf.at[left], sib)
        ops[1].wait_recv()
        two = copy(buf.at[right, dn], buf.at[right, dn], hl)
        sib_r = copy(buf.at[right], buf.at[right], sib)
        return one, two, ops[2], sib_l, sib_r

    def gather_end(buf, ops):
        opp = 2 * ring(h, 2) + c
        ops[0].wait_recv()
        ops[1].wait_recv()
        last = copy(buf.at[opp], buf.at[opp], sib)
        for op in ops[2:]:
            op.wait_recv()
        last.wait_recv()

    x20 = gather_start(x2all.at[0])
    lp_w.wait_recv()
    lp_y = [copy(lpn.at[rows64], lpn.at[rows64], dev(y=ring(y, o))) for o in (1, 2, 3)]
    duo = product(1, 0, 0)
    add_cores(duo + product(1, 0, 1))
    rs10 = reduce_start(1, 0)
    relay(0, 1, rs01)
    duo = product(1, 1, 0)
    add_cores(duo + product(1, 1, 1))
    rs11 = reduce_start(1, 1)
    share(1)
    place_20.pass_x()
    place_20.pass_z()
    x20 = gather_mid(x2all.at[0], x20)
    relay(1, 0, rs10)

    own8 = pl.ds(pl.multiple_of(zi * 8, 8), 8)

    class Chain:
        def __init__(self, red, ry, yr, rz, zr, gz, fin):
            self.bufs = (red, ry, yr, rz, zr, gz, fin)

        def y_start(self):
            red, ry = self.bufs[:2]
            self.ops = []
            for o in (1, 2, 3):
                to = ring(y, o)
                part = pl.ds(pl.multiple_of(to * 64, 64), 64)
                self.ops.append(copy(red.at[:, part], ry.at[o - 1], dev(y=to)))

        def z_start(self):
            red, ry, yr, rz = self.bufs[:4]
            acc = red[:, rows64, :]
            for o in range(3):
                self.ops[o].wait_recv()
                acc = acc + ry[o]
            yr[...] = acc
            self.ops = []
            for o in range(1, 8):
                to = ring(zi, o, 8)
                part = pl.ds(pl.multiple_of(to * 8, 8), 8)
                self.ops.append(copy(yr.at[:, part], rz.at[o - 1], zdev(to)))

        def plane_start(self, less=None):
            yr, rz, zr, gz = self.bufs[2:6]
            acc = yr[:, own8, :]
            for o in range(7):
                self.ops[o].wait_recv()
                acc = acc + rz[o]
            zr[...] = acc if less is None else acc - less[None]
            self.base = take(8)
            self.sends = []
            for v in (0, 1):
                op = copy(
                    zr, gz.at[:, own8], dev(k=h, w=v), recv=self.base + zi, start=False
                )
                self.sends.append(op)

                @pl.when(2 * h + v != zi)
                def _(op=op):
                    op.start()

        def x_send(self):
            zr, gz = self.bufs[4:6]
            got = ids[0]
            self.spread = [
                copy(gz, gz, dev(h=ring(h, o)), recv=got, start=False) for o in (1, 2, 3)
            ]

            @pl.when(h == k)
            def _():
                gz[:, own8, :] = zr[...]
                for o in range(1, 8):
                    frm = ring(zi, o, 8)
                    part = pl.ds(pl.multiple_of(frm * 8, 8), 8)
                    arrival(gz.at[:, part], self.base + frm).wait_recv()
                for op in self.spread:
                    op.start()

        def x_recv(self):
            @pl.when(h != k)
            def _():
                self.spread[0].wait_recv()

        def y_spread(self):
            gz, fin = self.bufs[5:]
            self.ops = [copy(gz, fin.at[:, rows64], dev(y=ring(y, o))) for o in (1, 2, 3)]
            fin[:, rows64, :] = gz[...]

        def finish(self):
            for op in self.ops:
                op.wait_recv()

        def drain(self):
            for v in (0, 1):

                @pl.when(2 * h + v != zi)
                def _(v=v):
                    self.sends[v].wait_send()

            @pl.when(h == k)
            def _():
                for op in self.spread:
                    op.wait_send()

    sum_g = Chain(red_g, ry_g, yr_g, rz_g, zr_g, gz_g, fin_g)
    sum_f = Chain(red_f, ry_f, yr_f, rz_f, zr_f, gz_f, fin_f)
    sum_s = Chain(red_s, ry_s, yr_s, rz_s, zr_s, gz_s, fin_s)
    x2_half(1, rs01)
    place_21.begin_x()
    place_21.begin_z()
    x21 = gather_start(x2all.at[1])
    red_g[0] = mm(lloc[0], x2[...], NT)
    sum_g.y_start()
    gather_end(x2all.at[0], x20)
    x21 = gather_mid(x2all.at[1], x21)
    relay(1, 1, rs11)
    sum_g.z_start()
    for op in lp_y:
        op.wait_recv()
    parent = par[n]
    lp_h, lp_l = split(lpn[...])
    d2c.wait_recv()
    here = jnp.where(parent == r, 1.0, 0.0)
    beside = jnp.where(parent == 2 * k + oc, 1.0, 0.0)
    own_rows = dot3(*split(d2[0, rows32] * here + d2s[0, rows32] * beside), lp_h, lp_l, NT)
    gather_end(x2all.at[1], x21)
    x2p = jnp.concatenate([x2all[0, parent], x2all[1, parent]], axis=1)
    red_f[0] = mm(x2p, lloc[1], NT)
    red_f[0, rows32] += own_rows
    sum_f.y_start()
    correction = dot3(lp_h, lp_l, *split(x2p))
    sum_g.plane_start()
    g_all[n] = zr_g[0]
    slices = [copy(g_all.at[n], g_all.at[n], sib)]
    for o in (1, 2, 3):
        for core in (c, oc):
            slices.append(copy(g_all.at[n], g_all.at[n], dev(h=ring(h, o), c=core)))
    sum_f.z_start()
    sum_g.x_send()
    x1[:, 0:128] = -total(1, 0, rs10) - correction[:, 0:128]
    x1[:, 128:256] = -total(1, 1, rs11) - correction[:, 128:256]
    place_10.begin_x()
    place_11.begin_x()
    red_s[0] = mm(lloc[1], x1[...], NT)
    sum_s.y_start()
    place_21.pass_x()
    place_21.pass_z()
    sum_g.x_recv()
    sum_g.y_spread()
    sum_s.z_start()
    for op in slices:
        op.wait_recv()
    sum_f.plane_start(dot3(*split(g_all[parent]), lp_h, lp_l, NT))
    sum_s.plane_start()
    place_10.begin_z()
    place_11.begin_z()
    place_10.pass_x()
    place_11.pass_x()
    sum_f.x_send()
    sum_s.x_send()
    sum_f.x_recv()
    sum_f.y_spread()
    sum_g.finish()
    g2o[...] = d2[0] - fin_g[0]
    sum_s.x_recv()
    sum_s.y_spread()
    place_10.pass_z()
    place_11.pass_z()
    sum_f.finish()
    pb = -fin_f[0]
    pbo[...] = pb
    update = d1[0] - mm(lpt[...], pb)
    sum_s.finish()
    g1o[...] = update - fin_s[0]
    place_20.finish()
    for move in (place_21, place_10, place_11):
        move.finish()

    for chain in (sum_g, sum_f, sum_s):
        chain.drain()

    @pl.when(h == k)
    def _():
        for op in lp_ops:
            op.wait_send()

    @pl.when(c == cy)
    def _():
        for op in l_ops:
            op.wait_send()

    for op in pending:
        op.wait_send()
    assert ids[0] <= SEMS


def settle(*refs):
    for src, dst in zip(refs[:5], refs[5:]):
        dst[...] = src[...].reshape(dst.shape)


def per_device(
    inverse_anc,
    lower_two,
    pattern_two,
    widths_two,
    dinv_two,
    lower_one,
    pattern_one,
    widths_one,
    parent_one,
    lower_par,
    dinv_one,
):
    vmem = pl.BlockSpec(memory_space=pltpu.VMEM)
    smem = pl.BlockSpec(memory_space=pltpu.SMEM)
    square = jax.ShapeDtypeStruct((B, B), F32)
    cube = jax.ShapeDtypeStruct((1, B, B), F32)

    def chain(count):
        return [
            pltpu.VMEM((count, B, B), F32),
            pltpu.VMEM((3, count, 64, B), F32),
            pltpu.VMEM((count, 64, B), F32),
            pltpu.VMEM((7, count, 8, B), F32),
            pltpu.VMEM((count, 8, B), F32),
            pltpu.VMEM((count, 64, B), F32),
            pltpu.VMEM((count, B, B), F32),
        ]

    outs = pl.pallas_call(
        kernel,
        out_shape=[square] * 5,
        in_specs=[smem] * 5 + [vmem] * 6,
        out_specs=[vmem] * 5,
        scratch_shapes=[
            pltpu.VMEM((3, 2, 1024, 128), F32),
            pltpu.VMEM((2, 64, 1024), F32),
            pltpu.VMEM((2, 8, 64, 1024), F32),
            pltpu.VMEM((2, 8, 64, 1024), BF16),
            pltpu.VMEM((2, 8, 64, 1024), BF16),
            pltpu.VMEM((2, 2, 1024, B), BF16),
            pltpu.VMEM((2, 2, 1024, B), BF16),
            pltpu.VMEM((2, 2, 4, 2, B, 128), F32),
            pltpu.VMEM((2, 2, 4, B, 128), F32),
            pltpu.VMEM((2, 2, 2, 128, 128), F32),
            pltpu.VMEM((2, 2, 2, 128, 128), F32),
            pltpu.VMEM((2, 2, 2, 128, 128), F32),
            pltpu.VMEM((2, 2, 2, 128, 128), F32),
            pltpu.VMEM((2, B, B), F32),
            pltpu.VMEM((2, B, B), F32),
            pltpu.VMEM((B, B), F32),
            pltpu.VMEM((B, B), F32),
            pltpu.VMEM((1, B, B), F32),
            pltpu.VMEM((2, 8, B, 128), F32),
            pltpu.VMEM((B, B), F32),
            pltpu.VMEM((B, B), F32),
            pltpu.VMEM((4, 4, 128, 128), F32),
            pltpu.VMEM((4, 4, 128, 128), F32),
            pltpu.VMEM((8, 8, B), F32),
            *chain(1),
            *chain(1),
            *chain(1),
            pltpu.SemaphoreType.DMA((SEMS,)),
            pltpu.SemaphoreType.DMA((SEMS,)),
        ],
        compiler_params=pltpu.CompilerParams(
            collective_id=0, has_side_effects=True, vmem_limit_bytes=56 * 1024 * 1024
        ),
    )(
        parent_one,
        widths_two,
        widths_one,
        pattern_two.T,
        pattern_one.T,
        inverse_anc,
        lower_two.T,
        lower_one.T,
        lower_par,
        dinv_two,
        dinv_one,
    )
    u2, g2, u1, pb, g1 = pl.pallas_call(
        settle,
        out_shape=[square, cube, square, cube, cube],
        in_specs=[vmem] * 5,
        out_specs=[vmem] * 5,
    )(outs[0], outs[2], outs[1], outs[3], outs[4])
    return u2, g2, u1, pb, g1


def solution(mesh):
    in_specs = (
        P("prow", "pcol"),
        P("prow", "pcol"),
        P(),
        P(),
        P("prow", None, None),
        P("prow", "pcol"),
        P(),
        P(),
        P(),
        P("prow", None, None),
        P("prow", None, None),
    )
    out_specs = (
        P("prow", "pcol"),
        P("prow", None, None),
        P("prow", "pcol"),
        P("prow", None, None),
        P("prow", None, None),
    )
    return jax.shard_map(
        per_device, mesh=mesh, in_specs=in_specs, out_specs=out_specs, check_vma=False
    )
```

```python
import functools

import jax
import jax.numpy as jnp
from jax import lax
from jax.experimental import pallas as pl
from jax.experimental.pallas import tpu as pltpu
from jax.sharding import PartitionSpec as P

B = 256
MESH = pl.DeviceIdType.MESH
F32 = jnp.float32
BF16 = jnp.bfloat16
NN = (((1,), (0,)), ((), ()))
NT = (((1,), (1,)), ((), ()))
SEMS = 300


def split(value):
    high = value.astype(BF16)
    return high, (value - high.astype(F32)).astype(BF16)


def dot3(lh, ll, rh, rl, dims=NN):
    dot = functools.partial(lax.dot_general, dimension_numbers=dims, preferred_element_type=F32)
    return dot(lh, rh) + (dot(lh, rl) + dot(ll, rh))


def mm(left, right, dims=NN):
    return dot3(*split(left), *split(right), dims)


def kernel(
    par, wid2, wid1, pat2, pat1, a_hbm, low2, low1, lpar, d2, d1,
    u2, u1, g2o, pbo, g1o,
    a, ag, lt, lg, lh, ll, ah, al, pp, rc, r_in, pl_in, f_in, s_out,
    lloc, lsnd, lpt, lpn, d2s, x2all, x2, x1, t_z, t_x, g_all,
    red_g, ry_g, yr_g, rz_g, zr_g, gz_g, fin_g,
    red_f, ry_f, yr_f, rz_f, zr_f, gz_f, fin_f,
    red_s, ry_s, yr_s, rz_s, zr_s, gz_s, fin_s,
    send_sem, recv_sem, load_sem,
):
    r, q = lax.axis_index("prow"), lax.axis_index("pcol")
    k, c = lax.div(r, 2), lax.rem(r, 2)
    h, y, w = lax.div(q, 8), lax.rem(lax.div(q, 2), 4), lax.rem(q, 2)
    zi = 2 * k + w
    oc = 1 - c
    n = 2 * h + c

    def dev(k=k, c=c, h=h, y=y, w=w):
        return (2 * k + c, 8 * h + 2 * y + w)

    def ring(v, off, size=4):
        return lax.rem(v + (off + size), size)

    def zdev(v):
        return dev(k=lax.div(v, 2), w=lax.rem(v, 2))

    ids = [0]
    pending = []

    def take(count):
        ids[0] += count
        return ids[0] - count

    def copy(src, dst, device, recv=None, start=True):
        num = take(1)
        op = pltpu.make_async_remote_copy(
            src_ref=src,
            dst_ref=dst,
            send_sem=send_sem.at[num],
            recv_sem=recv_sem.at[num if recv is None else recv],
            device_id=device,
            device_id_type=MESH,
        )
        if start:
            op.start()
            pending.append(op)
        return op

    def arrival(dst, recv):
        return pltpu.make_async_remote_copy(
            src_ref=dst,
            dst_ref=dst,
            send_sem=send_sem.at[0],
            recv_sem=recv_sem.at[recv],
            device_id=dev(c=oc),
            device_id_type=MESH,
        )

    barrier = pltpu.get_barrier_semaphore()
    friends = [dev(c=oc)]
    friends += [dev(h=ring(h, o)) for o in (1, 2, 3)]
    friends += [dev(y=ring(y, o)) for o in (1, 2, 3)]
    friends += [zdev(ring(zi, o, 8)) for o in range(1, 8)]
    friends += [dev(h=ring(h, o), c=oc) for o in (1, 2, 3)]
    for friend in friends:
        pl.semaphore_signal(barrier, inc=1, device_id=friend, device_id_type=MESH)

    load = pltpu.make_async_copy(a_hbm, a, load_sem)
    load.start()
    owner = lax.div(q, 4)
    inner = lax.rem(q, 4) * 64 + lax.broadcasted_iota(jnp.int32, (64, 1024), 0)
    block = lax.broadcasted_iota(jnp.int32, (64, 1024), 1) // B
    for lev, (low, pat, wid) in enumerate(((low2, pat2, wid2), (low1, pat1, wid1))):
        present = jnp.zeros((64, 1024), F32)
        for b in range(4):
            there = pat[owner, 4 * r + b].astype(F32)
            present = jnp.where(block == b, there, present)
        keep = jnp.where(inner < wid[owner], present, 0.0)
        lt[lev] = low[...] * keep
    row = lax.broadcasted_iota(jnp.int32, (B, B), 0)
    col = lax.broadcasted_iota(jnp.int32, (B, B), 1)
    inside = jnp.where(row < wid1[r], 1.0, 0.0) * jnp.where(col < wid2[par[r]], 1.0, 0.0)
    lpt[...] = lpar[0].T * inside

    load.wait()
    pl.semaphore_wait(barrier, len(friends))

    hl, hr = dev(h=ring(h, -1)), dev(h=ring(h, 1))
    yl, yr = dev(y=ring(y, -1)), dev(y=ring(y, 1))
    sib, pair = dev(c=oc), dev(w=1 - w)
    mine = 2 * y + w
    theirs = 2 * y + 1 - w
    ml, mr, mf = 2 * ring(y, -1), 2 * ring(y, 1), 2 * ring(y, 2)
    top, bot = pl.ds(0, 512), pl.ds(512, 512)

    def split_l(lev, m):
        hi, lo = split(lg[lev, m])
        lh[lev, m] = hi
        ll[lev, m] = lo

    def send_own(lev):
        return (
            copy(lt.at[lev], lg.at[lev, mine], yr),
            copy(lt.at[lev], lg.at[lev, mine], yl),
        )

    def send_pair(lev):
        return (
            copy(lg.at[lev, theirs], lg.at[lev, theirs], yr),
            copy(lg.at[lev, theirs], lg.at[lev, theirs], yl),
        )

    def forward_l(lev, ops, which):
        near, far = pl.ds(0, 32), pl.ds(32, 32)
        ops[0].wait_recv()
        one = copy(lg.at[lev, ml + which, near], lg.at[lev, ml + which, near], yr)
        ops[1].wait_recv()
        two = copy(lg.at[lev, mr + which, far], lg.at[lev, mr + which, far], yl)
        return one, two

    def send_a(half):
        cols = pl.ds(128 * half, 128)
        return (
            copy(a.at[top, cols], ag.at[0, half, top], hr),
            copy(a.at[bot, cols], ag.at[1, half, bot], hl),
            copy(a.at[bot, cols], ag.at[0, half, bot], hr),
            copy(a.at[top, cols], ag.at[1, half, top], hl),
        )

    def forward_a(half, ops):
        ops[0].wait_recv()
        one = copy(ag.at[0, half, top], ag.at[2, half, top], hr)
        ops[1].wait_recv()
        two = copy(ag.at[1, half, bot], ag.at[2, half, bot], hl)
        return one, two

    def split_a(half, rel):
        hi, lo = split(a[:, 128 * half : 128 * half + 128] if rel == 0 else ag[rel - 1, half])
        cols = slice(128 * (rel % 2), 128 * (rel % 2) + 128)
        ah[half, rel // 2, :, cols] = hi
        al[half, rel // 2, :, cols] = lo

    w2 = copy(lt.at[0], lg.at[0, mine], pair)
    o2 = send_own(0)
    a0 = send_a(0)
    d2c = copy(d2, d2s, sib)

    rows32 = pl.ds(pl.multiple_of(mine * 32, 32), 32)
    rows64 = pl.ds(pl.multiple_of(y * 64, 64), 64)
    lp_recv = ids[0]
    lp_ops = [
        copy(lpt.at[rows32], lpn.at[rows32], dev(k=ring(k, o)), recv=lp_recv, start=False)
        for o in (1, 2, 3)
    ]

    @pl.when(h == k)
    def _():
        lpn[rows32] = lpt[rows32]
        for op in lp_ops:
            op.start()

    lg[0, mine] = lt[0]
    lg[1, mine] = lt[1]
    split_l(0, mine)
    split_l(1, mine)
    split_a(0, 0)
    split_a(1, 0)
    w2.wait_recv()
    p2 = send_pair(0)
    f2 = forward_l(0, o2, w)
    split_l(0, theirs)
    split_l(0, ml + w)
    split_l(0, mr + w)
    fa0 = forward_a(0, a0)
    a1 = send_a(1)
    w1 = copy(lt.at[1], lg.at[1, mine], pair)
    e2 = forward_l(0, p2, 1 - w)
    o1 = send_own(1)
    split_l(0, ml + 1 - w)
    split_l(0, mr + 1 - w)
    a0[2].wait_recv()
    split_a(0, 1)
    a0[3].wait_recv()
    split_a(0, 2)
    for op in f2:
        op.wait_recv()
    split_l(0, mf + w)
    for op in e2:
        op.wait_recv()
    split_l(0, mf + 1 - w)

    cy = lax.div(y, 2)
    off = pl.multiple_of(lax.rem(mine, 4) * B, B)
    l_ops = [copy(lsnd.at[lev], lloc.at[lev], sib, start=False) for lev in range(2)]

    def share(lev):
        @pl.when(c == cy)
        def _():
            lsnd[lev] = lg[lev, pl.ds(4 * oc, 4), :, pl.ds(off, B)].reshape(B, B)
            l_ops[lev].start()
            lloc[lev] = lg[lev, pl.ds(4 * c, 4), :, pl.ds(off, B)].reshape(B, B)

        @pl.when(c != cy)
        def _():
            l_ops[lev].wait_recv()

    kp, km, ko = ring(k, 1), ring(k, -1), ring(k, 2)
    zp, zm = dev(k=kp), dev(k=km)
    up, dn = pl.ds(0, 128), pl.ds(128, 128)
    slots = (h, ring(h, -1), ring(h, 1), ring(h, 2))

    def product(lev, half, duo):
        def part(parity):
            left_h = lh[lev, pl.ds(4 * parity, 4)].reshape(B, 1024)
            left_l = ll[lev, pl.ds(4 * parity, 4)].reshape(B, 1024)
            value = dot3(left_h, left_l, ah[half, duo], al[half, duo])
            for side in range(2):
                pp[lev, half, slots[2 * duo + side], parity] = value[:, 128 * side : 128 * side + 128]

        part(oc)
        ops = []
        for side in range(2):
            slot = slots[2 * duo + side]
            ops.append(copy(pp.at[lev, half, slot, oc], rc.at[lev, half, slot], sib))
        part(c)
        return [(lev, half, slots[2 * duo + side], ops[side]) for side in range(2)]

    def add_cores(parts):
        for lev, half, slot, op in parts:
            op.wait_recv()
            pp[lev, half, slot, c] += rc[lev, half, slot]

    def reduce_start(lev, half):
        mine_of = pp.at[lev, half]
        return [
            copy(mine_of.at[ko, c, up], r_in.at[lev, half, 0], zp),
            copy(mine_of.at[ko, c, dn], r_in.at[lev, half, 1], zm),
            copy(mine_of.at[kp, c, dn], pl_in.at[lev, half, 0], zp),
            copy(mine_of.at[km, c, up], pl_in.at[lev, half, 1], zm),
        ]

    def relay(lev, half, ops):
        ops[0].wait_recv()
        s_out[lev, half, 0] = r_in[lev, half, 0] + pp[lev, half, kp, c, up]
        ops.append(copy(s_out.at[lev, half, 0], f_in.at[lev, half, 0], zp))
        ops[1].wait_recv()
        s_out[lev, half, 1] = r_in[lev, half, 1] + pp[lev, half, km, c, dn]
        ops.append(copy(s_out.at[lev, half, 1], f_in.at[lev, half, 1], zm))

    def total(lev, half, ops):
        for op in ops[2:]:
            op.wait_recv()
        upper = pp[lev, half, k, c, up] + f_in[lev, half, 0] + pl_in[lev, half, 1]
        lower = pp[lev, half, k, c, dn] + f_in[lev, half, 1] + pl_in[lev, half, 0]
        return jnp.concatenate([upper, lower], axis=0)

    class Place:
        def __init__(self, piece, buf, out):
            tz, tx = t_z.at[piece], t_x.at[piece]
            self.buf, self.out, self.tz, self.tx = buf, out, tz, tx
            self.z_base, self.x_base = take(4), take(4)
            self.got_z, self.got_x = take(1), take(1)
            self.via_z = copy(
                buf.at[up], tz.at[k], dev(k=h), recv=self.z_base + ring(k, 4 - h), start=False
            )
            self.via_x = copy(
                buf.at[dn], tx.at[h], dev(h=k), recv=self.x_base + ring(h, 4 - k), start=False
            )
            self.on_z, self.on_x = [], []
            for o in (1, 2, 3):
                v = ring(k, o)
                self.on_z.append(
                    copy(tz.at[v], out.at[up], dev(h=v), recv=self.got_z, start=False)
                )
                self.on_x.append(
                    copy(tx.at[v], out.at[dn], dev(k=v), recv=self.got_x, start=False)
                )

        def begin_x(self):
            @pl.when(h != k)
            def _():
                self.via_x.start()

            @pl.when(h == k)
            def _():
                self.out[...] = self.buf[...]

        def begin_z(self):
            @pl.when(h != k)
            def _():
                self.via_z.start()

        def pass_x(self):
            @pl.when(h == k)
            def _():
                for o in (2, 1, 3):
                    arrival(self.tx.at[ring(k, o)], self.x_base + o).wait_recv()
                    self.on_x[o - 1].start()

        def pass_z(self):
            @pl.when(h == k)
            def _():
                for o in (2, 1, 3):
                    arrival(self.tz.at[ring(k, o)], self.z_base + o).wait_recv()
                    self.on_z[o - 1].start()

        def finish(self):
            @pl.when(h != k)
            def _():
                self.via_z.wait_send()
                self.via_x.wait_send()
                arrival(self.out.at[up], self.got_z).wait_recv()
                arrival(self.out.at[dn], self.got_x).wait_recv()

            @pl.when(h == k)
            def _():
                for op in self.on_z + self.on_x:
                    op.wait_send()

    left, right = pl.ds(0, 128), pl.ds(128, 128)
    place_20 = Place(0, x2.at[:, left], u2.at[:, left])
    place_21 = Place(1, x2.at[:, right], u2.at[:, right])
    place_10 = Place(2, x1.at[:, left], u1.at[:, left])
    place_11 = Place(3, x1.at[:, right], u1.at[:, right])

    def x2_half(half, ops):
        value = -total(0, half, ops)
        x2[:, 128 * half : 128 * half + 128] = value
        x2all[half, n] = value

    duo = product(0, 0, 0)
    for op in fa0:
        op.wait_recv()
    split_a(0, 3)
    add_cores(duo + product(0, 0, 1))
    rs00 = reduce_start(0, 0)
    fa1 = forward_a(1, a1)
    share(0)
    w1.wait_recv()
    p1 = send_pair(1)
    f1 = forward_l(1, o1, w)
    split_l(1, theirs)
    split_l(1, ml + w)
    split_l(1, mr + w)
    relay(0, 0, rs00)
    e1 = forward_l(1, p1, 1 - w)

    @pl.when(h != k)
    def _():
        lp_ops[0].wait_recv()

    lp_w = copy(lpn.at[rows32], lpn.at[rows32], pair)
    split_l(1, ml + 1 - w)
    split_l(1, mr + 1 - w)
    a1[2].wait_recv()
    split_a(1, 1)
    a1[3].wait_recv()
    split_a(1, 2)
    duo = product(0, 1, 0)
    for op in f1:
        op.wait_recv()
    split_l(1, mf + w)
    x2_half(0, rs00)
    place_20.begin_x()
    place_20.begin_z()
    for op in fa1:
        op.wait_recv()
    split_a(1, 3)
    add_cores(duo + product(0, 1, 1))
    rs01 = reduce_start(0, 1)
    for op in e1:
        op.wait_recv()
    split_l(1, mf + 1 - w)

    def gather_start(buf):
        return copy(buf.at[n], buf.at[n], hr), copy(buf.at[n], buf.at[n], hl), copy(
            buf.at[n], buf.at[n], sib
        )

    def gather_mid(buf, ops):
        left, right = 2 * ring(h, -1) + c, 2 * ring(h, 1) + c
        ops[0].wait_recv()
        one = copy(buf.at[left, up], buf.at[left, up], hr)
        sib_l = copy(buf.at[left], buf.at[left], sib)
        ops[1].wait_recv()
        two = copy(buf.at[right, dn], buf.at[right, dn], hl)
        sib_r = copy(buf.at[right], buf.at[right], sib)
        return one, two, ops[2], sib_l, sib_r

    def gather_end(buf, ops):
        opp = 2 * ring(h, 2) + c
        ops[0].wait_recv()
        ops[1].wait_recv()
        last = copy(buf.at[opp], buf.at[opp], sib)
        for op in ops[2:]:
            op.wait_recv()
        last.wait_recv()

    x20 = gather_start(x2all.at[0])
    lp_w.wait_recv()
    lp_y = [copy(lpn.at[rows64], lpn.at[rows64], dev(y=ring(y, o))) for o in (1, 2, 3)]
    duo = product(1, 0, 0)
    add_cores(duo + product(1, 0, 1))
    rs10 = reduce_start(1, 0)
    relay(0, 1, rs01)
    duo = product(1, 1, 0)
    add_cores(duo + product(1, 1, 1))
    rs11 = reduce_start(1, 1)
    share(1)
    place_20.pass_x()
    place_20.pass_z()
    x20 = gather_mid(x2all.at[0], x20)
    relay(1, 0, rs10)

    own8 = pl.ds(pl.multiple_of(zi * 8, 8), 8)

    class Chain:
        def __init__(self, red, ry, yr, rz, zr, gz, fin):
            self.bufs = (red, ry, yr, rz, zr, gz, fin)

        def y_start(self):
            red, ry = self.bufs[:2]
            self.ops = []
            for o in (1, 2, 3):
                to = ring(y, o)
                part = pl.ds(pl.multiple_of(to * 64, 64), 64)
                self.ops.append(copy(red.at[:, part], ry.at[o - 1], dev(y=to)))

        def z_start(self):
            red, ry, yr, rz = self.bufs[:4]
            acc = red[:, rows64, :]
            for o in range(3):
                self.ops[o].wait_recv()
                acc = acc + ry[o]
            yr[...] = acc
            self.ops = []
            for o in range(1, 8):
                to = ring(zi, o, 8)
                part = pl.ds(pl.multiple_of(to * 8, 8), 8)
                self.ops.append(copy(yr.at[:, part], rz.at[o - 1], zdev(to)))

        def plane_start(self, less=None):
            yr, rz, zr, gz = self.bufs[2:6]
            acc = yr[:, own8, :]
            for o in range(7):
                self.ops[o].wait_recv()
                acc = acc + rz[o]
            zr[...] = acc if less is None else acc - less[None]
            self.base = take(8)
            self.sends = []
            for v in (0, 1):
                op = copy(
                    zr, gz.at[:, own8], dev(k=h, w=v), recv=self.base + zi, start=False
                )
                self.sends.append(op)

                @pl.when(2 * h + v != zi)
                def _(op=op):
                    op.start()

        def x_send(self):
            zr, gz = self.bufs[4:6]
            got = ids[0]
            self.spread = [
                copy(gz, gz, dev(h=ring(h, o)), recv=got, start=False) for o in (1, 2, 3)
            ]

            @pl.when(h == k)
            def _():
                gz[:, own8, :] = zr[...]
                for o in range(1, 8):
                    frm = ring(zi, o, 8)
                    part = pl.ds(pl.multiple_of(frm * 8, 8), 8)
                    arrival(gz.at[:, part], self.base + frm).wait_recv()
                for op in self.spread:
                    op.start()

        def x_recv(self):
            @pl.when(h != k)
            def _():
                self.spread[0].wait_recv()

        def y_spread(self):
            gz, fin = self.bufs[5:]
            self.ops = [copy(gz, fin.at[:, rows64], dev(y=ring(y, o))) for o in (1, 2, 3)]
            fin[:, rows64, :] = gz[...]

        def finish(self):
            for op in self.ops:
                op.wait_recv()

        def drain(self):
            for v in (0, 1):

                @pl.when(2 * h + v != zi)
                def _(v=v):
                    self.sends[v].wait_send()

            @pl.when(h == k)
            def _():
                for op in self.spread:
                    op.wait_send()

    sum_g = Chain(red_g, ry_g, yr_g, rz_g, zr_g, gz_g, fin_g)
    sum_f = Chain(red_f, ry_f, yr_f, rz_f, zr_f, gz_f, fin_f)
    sum_s = Chain(red_s, ry_s, yr_s, rz_s, zr_s, gz_s, fin_s)
    x2_half(1, rs01)
    place_21.begin_x()
    place_21.begin_z()
    x21 = gather_start(x2all.at[1])
    red_g[0] = mm(lloc[0], x2[...], NT)
    sum_g.y_start()
    gather_end(x2all.at[0], x20)
    x21 = gather_mid(x2all.at[1], x21)
    relay(1, 1, rs11)
    sum_g.z_start()
    for op in lp_y:
        op.wait_recv()
    parent = par[n]
    lp_h, lp_l = split(lpn[...])
    d2c.wait_recv()
    here = jnp.where(parent == r, 1.0, 0.0)
    beside = jnp.where(parent == 2 * k + oc, 1.0, 0.0)
    own_rows = dot3(*split(d2[0, rows32] * here + d2s[0, rows32] * beside), lp_h, lp_l, NT)
    gather_end(x2all.at[1], x21)
    x2p = jnp.concatenate([x2all[0, parent], x2all[1, parent]], axis=1)
    red_f[0] = mm(x2p, lloc[1], NT)
    red_f[0, rows32] += own_rows
    sum_f.y_start()
    correction = dot3(lp_h, lp_l, *split(x2p))
    sum_g.plane_start()
    g_all[n] = zr_g[0]
    slices = [copy(g_all.at[n], g_all.at[n], sib)]
    for o in (1, 2, 3):
        for core in (c, oc):
            slices.append(copy(g_all.at[n], g_all.at[n], dev(h=ring(h, o), c=core)))
    sum_f.z_start()
    sum_g.x_send()
    x1[:, 0:128] = -total(1, 0, rs10) - correction[:, 0:128]
    place_10.begin_x()
    place_10.begin_z()
    x1[:, 128:256] = -total(1, 1, rs11) - correction[:, 128:256]
    place_11.begin_x()
    red_s[0] = mm(lloc[1], x1[...], NT)
    sum_s.y_start()
    place_21.pass_x()
    place_21.pass_z()
    for op in slices:
        op.wait_recv()
    sum_f.plane_start(dot3(*split(g_all[parent]), lp_h, lp_l, NT))
    sum_g.x_recv()
    sum_g.y_spread()
    sum_s.z_start()
    sum_f.x_send()
    sum_s.plane_start()
    place_10.pass_x()
    place_11.begin_z()
    place_11.pass_x()
    sum_s.x_send()
    sum_f.x_recv()
    sum_f.y_spread()
    sum_g.finish()
    g2o[...] = d2[0] - fin_g[0]
    sum_s.x_recv()
    sum_s.y_spread()
    place_10.pass_z()
    place_11.pass_z()
    sum_f.finish()
    pb = -fin_f[0]
    pbo[...] = pb
    update = d1[0] - mm(lpt[...], pb)
    sum_s.finish()
    g1o[...] = update - fin_s[0]
    place_20.finish()
    for move in (place_21, place_10, place_11):
        move.finish()

    for chain in (sum_g, sum_f, sum_s):
        chain.drain()

    @pl.when(h == k)
    def _():
        for op in lp_ops:
            op.wait_send()

    @pl.when(c == cy)
    def _():
        for op in l_ops:
            op.wait_send()

    for op in pending:
        op.wait_send()
    assert ids[0] <= SEMS


def settle(*refs):
    held, in_sem, out_sem = refs[10:]
    loads, stores = [], []
    for num in range(5):
        loads.append(pltpu.make_async_copy(refs[num], held.at[num], in_sem.at[num]))
        loads[-1].start()
    for num in range(5):
        dst = refs[5 + num]
        to = dst.at[0] if len(dst.shape) == 3 else dst
        stores.append(pltpu.make_async_copy(held.at[num], to, out_sem.at[num]))
        loads[num].wait()
        stores[-1].start()
    for op in stores:
        op.wait()


def per_device(
    inverse_anc,
    lower_two,
    pattern_two,
    widths_two,
    dinv_two,
    lower_one,
    pattern_one,
    widths_one,
    parent_one,
    lower_par,
    dinv_one,
):
    vmem = pl.BlockSpec(memory_space=pltpu.VMEM)
    smem = pl.BlockSpec(memory_space=pltpu.SMEM)
    square = jax.ShapeDtypeStruct((B, B), F32)
    cube = jax.ShapeDtypeStruct((1, B, B), F32)

    def chain(count):
        return [
            pltpu.VMEM((count, B, B), F32),
            pltpu.VMEM((3, count, 64, B), F32),
            pltpu.VMEM((count, 64, B), F32),
            pltpu.VMEM((7, count, 8, B), F32),
            pltpu.VMEM((count, 8, B), F32),
            pltpu.VMEM((count, 64, B), F32),
            pltpu.VMEM((count, B, B), F32),
        ]

    outs = pl.pallas_call(
        kernel,
        out_shape=[square] * 5,
        in_specs=[smem] * 5 + [pl.BlockSpec(memory_space=pl.ANY)] + [vmem] * 5,
        out_specs=[vmem] * 5,
        scratch_shapes=[
            pltpu.VMEM((1024, B), F32),
            pltpu.VMEM((3, 2, 1024, 128), F32),
            pltpu.VMEM((2, 64, 1024), F32),
            pltpu.VMEM((2, 8, 64, 1024), F32),
            pltpu.VMEM((2, 8, 64, 1024), BF16),
            pltpu.VMEM((2, 8, 64, 1024), BF16),
            pltpu.VMEM((2, 2, 1024, B), BF16),
            pltpu.VMEM((2, 2, 1024, B), BF16),
            pltpu.VMEM((2, 2, 4, 2, B, 128), F32),
            pltpu.VMEM((2, 2, 4, B, 128), F32),
            pltpu.VMEM((2, 2, 2, 128, 128), F32),
            pltpu.VMEM((2, 2, 2, 128, 128), F32),
            pltpu.VMEM((2, 2, 2, 128, 128), F32),
            pltpu.VMEM((2, 2, 2, 128, 128), F32),
            pltpu.VMEM((2, B, B), F32),
            pltpu.VMEM((2, B, B), F32),
            pltpu.VMEM((B, B), F32),
            pltpu.VMEM((B, B), F32),
            pltpu.VMEM((1, B, B), F32),
            pltpu.VMEM((2, 8, B, 128), F32),
            pltpu.VMEM((B, B), F32),
            pltpu.VMEM((B, B), F32),
            pltpu.VMEM((4, 4, 128, 128), F32),
            pltpu.VMEM((4, 4, 128, 128), F32),
            pltpu.VMEM((8, 8, B), F32),
            *chain(1),
            *chain(1),
            *chain(1),
            pltpu.SemaphoreType.DMA((SEMS,)),
            pltpu.SemaphoreType.DMA((SEMS,)),
            pltpu.SemaphoreType.DMA,
        ],
        compiler_params=pltpu.CompilerParams(
            collective_id=0, has_side_effects=True, vmem_limit_bytes=56 * 1024 * 1024
        ),
    )(
        parent_one,
        widths_two,
        widths_one,
        pattern_two.T,
        pattern_one.T,
        inverse_anc,
        lower_two.T,
        lower_one.T,
        lower_par,
        dinv_two,
        dinv_one,
    )
    u2, g2, u1, pb, g1 = pl.pallas_call(
        settle,
        out_shape=[square, cube, square, cube, cube],
        in_specs=[pl.BlockSpec(memory_space=pl.ANY)] * 5,
        out_specs=[pl.BlockSpec(memory_space=pl.ANY)] * 5,
        scratch_shapes=[
            pltpu.VMEM((5, B, B), F32),
            pltpu.SemaphoreType.DMA((5,)),
            pltpu.SemaphoreType.DMA((5,)),
        ],
    )(outs[0], outs[2], outs[1], outs[3], outs[4])
    return u2, g2, u1, pb, g1


def solution(mesh):
    in_specs = (
        P("prow", "pcol"),
        P("prow", "pcol"),
        P(),
        P(),
        P("prow", None, None),
        P("prow", "pcol"),
        P(),
        P(),
        P(),
        P("prow", None, None),
        P("prow", None, None),
    )
    out_specs = (
        P("prow", "pcol"),
        P("prow", None, None),
        P("prow", "pcol"),
        P("prow", None, None),
        P("prow", None, None),
    )
    return jax.shard_map(
        per_device, mesh=mesh, in_specs=in_specs, out_specs=out_specs, check_vma=False
    )
```

```python
import functools

import jax
import jax.numpy as jnp
from jax import lax
from jax.experimental import pallas as pl
from jax.experimental.pallas import tpu as pltpu
from jax.sharding import PartitionSpec as P

B = 256
MESH = pl.DeviceIdType.MESH
F32 = jnp.float32
BF16 = jnp.bfloat16
NN = (((1,), (0,)), ((), ()))
NT = (((1,), (1,)), ((), ()))
SEMS = 300


def split(value):
    high = value.astype(BF16)
    return high, (value - high.astype(F32)).astype(BF16)


def dot3(lh, ll, rh, rl, dims=NN):
    dot = functools.partial(lax.dot_general, dimension_numbers=dims, preferred_element_type=F32)
    return dot(lh, rh) + (dot(lh, rl) + dot(ll, rh))


def mm(left, right, dims=NN):
    return dot3(*split(left), *split(right), dims)


def kernel(
    par, wid2, wid1, pat2, pat1, a_hbm, low2, low1, lpar, d2, d1,
    u2, u1, g2o, pbo, g1o,
    a, ag, lt, lg, lh, ll, ah, al, pp, rc, r_in, pl_in, f_in, s_out,
    lloc, lsnd, lpt, lpn, d2s, x2all, x2, x1, t_z, t_x, g_all,
    red_g, ry_g, yr_g, rz_g, zr_g, gz_g, fin_g,
    red_f, ry_f, yr_f, rz_f, zr_f, gz_f, fin_f,
    red_s, ry_s, yr_s, rz_s, zr_s, gz_s, fin_s,
    send_sem, recv_sem, load_sem,
):
    r, q = lax.axis_index("prow"), lax.axis_index("pcol")
    k, c = lax.div(r, 2), lax.rem(r, 2)
    h, y, w = lax.div(q, 8), lax.rem(lax.div(q, 2), 4), lax.rem(q, 2)
    zi = 2 * k + w
    oc = 1 - c
    n = 2 * h + c

    def dev(k=k, c=c, h=h, y=y, w=w):
        return (2 * k + c, 8 * h + 2 * y + w)

    def ring(v, off, size=4):
        return lax.rem(v + (off + size), size)

    def zdev(v):
        return dev(k=lax.div(v, 2), w=lax.rem(v, 2))

    ids = [0]
    pending = []

    def take(count):
        ids[0] += count
        return ids[0] - count

    def copy(src, dst, device, recv=None, start=True):
        num = take(1)
        op = pltpu.make_async_remote_copy(
            src_ref=src,
            dst_ref=dst,
            send_sem=send_sem.at[num],
            recv_sem=recv_sem.at[num if recv is None else recv],
            device_id=device,
            device_id_type=MESH,
        )
        if start:
            op.start()
            pending.append(op)
        return op

    def arrival(dst, recv):
        return pltpu.make_async_remote_copy(
            src_ref=dst,
            dst_ref=dst,
            send_sem=send_sem.at[0],
            recv_sem=recv_sem.at[recv],
            device_id=dev(c=oc),
            device_id_type=MESH,
        )

    barrier = pltpu.get_barrier_semaphore()
    friends = [dev(c=oc)]
    friends += [dev(h=ring(h, o)) for o in (1, 2, 3)]
    friends += [dev(y=ring(y, o)) for o in (1, 2, 3)]
    friends += [zdev(ring(zi, o, 8)) for o in range(1, 8)]
    friends += [dev(h=ring(h, o), c=oc) for o in (1, 2, 3)]
    for friend in friends:
        pl.semaphore_signal(barrier, inc=1, device_id=friend, device_id_type=MESH)

    load = pltpu.make_async_copy(a_hbm, a, load_sem)
    load.start()
    owner = lax.div(q, 4)
    inner = lax.rem(q, 4) * 64 + lax.broadcasted_iota(jnp.int32, (64, 1024), 0)
    block = lax.broadcasted_iota(jnp.int32, (64, 1024), 1) // B
    for lev, (low, pat, wid) in enumerate(((low2, pat2, wid2), (low1, pat1, wid1))):
        present = jnp.zeros((64, 1024), F32)
        for b in range(4):
            there = pat[owner, 4 * r + b].astype(F32)
            present = jnp.where(block == b, there, present)
        keep = jnp.where(inner < wid[owner], present, 0.0)
        lt[lev] = low[...] * keep
    row = lax.broadcasted_iota(jnp.int32, (B, B), 0)
    col = lax.broadcasted_iota(jnp.int32, (B, B), 1)
    inside = jnp.where(row < wid1[r], 1.0, 0.0) * jnp.where(col < wid2[par[r]], 1.0, 0.0)
    lpt[...] = lpar[0].T * inside

    load.wait()
    pl.semaphore_wait(barrier, len(friends))

    hl, hr = dev(h=ring(h, -1)), dev(h=ring(h, 1))
    yl, yr = dev(y=ring(y, -1)), dev(y=ring(y, 1))
    sib, pair = dev(c=oc), dev(w=1 - w)
    mine = 2 * y + w
    theirs = 2 * y + 1 - w
    ml, mr, mf = 2 * ring(y, -1), 2 * ring(y, 1), 2 * ring(y, 2)
    top, bot = pl.ds(0, 512), pl.ds(512, 512)

    def split_l(lev, m):
        hi, lo = split(lg[lev, m])
        lh[lev, m] = hi
        ll[lev, m] = lo

    def send_own(lev):
        return (
            copy(lt.at[lev], lg.at[lev, mine], yr),
            copy(lt.at[lev], lg.at[lev, mine], yl),
        )

    def send_pair(lev):
        return (
            copy(lg.at[lev, theirs], lg.at[lev, theirs], yr),
            copy(lg.at[lev, theirs], lg.at[lev, theirs], yl),
        )

    def forward_l(lev, ops, which):
        near, far = pl.ds(0, 32), pl.ds(32, 32)
        ops[0].wait_recv()
        one = copy(lg.at[lev, ml + which, near], lg.at[lev, ml + which, near], yr)
        ops[1].wait_recv()
        two = copy(lg.at[lev, mr + which, far], lg.at[lev, mr + which, far], yl)
        return one, two

    def send_a(half):
        cols = pl.ds(128 * half, 128)
        return (
            copy(a.at[top, cols], ag.at[0, half, top], hr),
            copy(a.at[bot, cols], ag.at[1, half, bot], hl),
            copy(a.at[bot, cols], ag.at[0, half, bot], hr),
            copy(a.at[top, cols], ag.at[1, half, top], hl),
        )

    def forward_a(half, ops):
        ops[0].wait_recv()
        one = copy(ag.at[0, half, top], ag.at[2, half, top], hr)
        ops[1].wait_recv()
        two = copy(ag.at[1, half, bot], ag.at[2, half, bot], hl)
        return one, two

    def split_a(half, rel):
        hi, lo = split(a[:, 128 * half : 128 * half + 128] if rel == 0 else ag[rel - 1, half])
        cols = slice(128 * (rel % 2), 128 * (rel % 2) + 128)
        ah[half, rel // 2, :, cols] = hi
        al[half, rel // 2, :, cols] = lo

    w2 = copy(lt.at[0], lg.at[0, mine], pair)
    o2 = send_own(0)
    a0 = send_a(0)
    d2c = copy(d2, d2s, sib)

    rows32 = pl.ds(pl.multiple_of(mine * 32, 32), 32)
    rows64 = pl.ds(pl.multiple_of(y * 64, 64), 64)
    lp_recv = ids[0]
    lp_ops = [
        copy(lpt.at[rows32], lpn.at[rows32], dev(k=ring(k, o)), recv=lp_recv, start=False)
        for o in (1, 2, 3)
    ]

    @pl.when(h == k)
    def _():
        lpn[rows32] = lpt[rows32]
        for op in lp_ops:
            op.start()

    lg[0, mine] = lt[0]
    lg[1, mine] = lt[1]
    split_l(0, mine)
    split_l(1, mine)
    split_a(0, 0)
    split_a(1, 0)
    w2.wait_recv()
    p2 = send_pair(0)
    f2 = forward_l(0, o2, w)
    split_l(0, theirs)
    split_l(0, ml + w)
    split_l(0, mr + w)
    fa0 = forward_a(0, a0)
    a1 = send_a(1)
    w1 = copy(lt.at[1], lg.at[1, mine], pair)
    e2 = forward_l(0, p2, 1 - w)
    o1 = send_own(1)
    split_l(0, ml + 1 - w)
    split_l(0, mr + 1 - w)
    a0[2].wait_recv()
    split_a(0, 1)
    a0[3].wait_recv()
    split_a(0, 2)
    for op in f2:
        op.wait_recv()
    split_l(0, mf + w)
    for op in e2:
        op.wait_recv()
    split_l(0, mf + 1 - w)

    cy = lax.div(y, 2)
    off = pl.multiple_of(lax.rem(mine, 4) * B, B)
    l_ops = [copy(lsnd.at[lev], lloc.at[lev], sib, start=False) for lev in range(2)]

    def share(lev):
        @pl.when(c == cy)
        def _():
            lsnd[lev] = lg[lev, pl.ds(4 * oc, 4), :, pl.ds(off, B)].reshape(B, B)
            l_ops[lev].start()
            lloc[lev] = lg[lev, pl.ds(4 * c, 4), :, pl.ds(off, B)].reshape(B, B)

        @pl.when(c != cy)
        def _():
            l_ops[lev].wait_recv()

    kp, km, ko = ring(k, 1), ring(k, -1), ring(k, 2)
    zp, zm = dev(k=kp), dev(k=km)
    up, dn = pl.ds(0, 128), pl.ds(128, 128)
    slots = (h, ring(h, -1), ring(h, 1), ring(h, 2))

    def product(lev, half, duo):
        def part(parity):
            left_h = lh[lev, pl.ds(4 * parity, 4)].reshape(B, 1024)
            left_l = ll[lev, pl.ds(4 * parity, 4)].reshape(B, 1024)
            value = dot3(left_h, left_l, ah[half, duo], al[half, duo])
            for side in range(2):
                pp[lev, half, slots[2 * duo + side], parity] = value[:, 128 * side : 128 * side + 128]

        part(oc)
        ops = []
        for side in range(2):
            slot = slots[2 * duo + side]
            ops.append(copy(pp.at[lev, half, slot, oc], rc.at[lev, half, slot], sib))
        part(c)
        return [(lev, half, slots[2 * duo + side], ops[side]) for side in range(2)]

    def add_cores(parts):
        for lev, half, slot, op in parts:
            op.wait_recv()
            pp[lev, half, slot, c] += rc[lev, half, slot]

    def reduce_start(lev, half):
        mine_of = pp.at[lev, half]
        return [
            copy(mine_of.at[ko, c, up], r_in.at[lev, half, 0], zp),
            copy(mine_of.at[ko, c, dn], r_in.at[lev, half, 1], zm),
            copy(mine_of.at[kp, c, dn], pl_in.at[lev, half, 0], zp),
            copy(mine_of.at[km, c, up], pl_in.at[lev, half, 1], zm),
        ]

    def relay(lev, half, ops):
        ops[0].wait_recv()
        s_out[lev, half, 0] = r_in[lev, half, 0] + pp[lev, half, kp, c, up]
        ops.append(copy(s_out.at[lev, half, 0], f_in.at[lev, half, 0], zp))
        ops[1].wait_recv()
        s_out[lev, half, 1] = r_in[lev, half, 1] + pp[lev, half, km, c, dn]
        ops.append(copy(s_out.at[lev, half, 1], f_in.at[lev, half, 1], zm))

    def total(lev, half, ops):
        for op in ops[2:]:
            op.wait_recv()
        upper = pp[lev, half, k, c, up] + f_in[lev, half, 0] + pl_in[lev, half, 1]
        lower = pp[lev, half, k, c, dn] + f_in[lev, half, 1] + pl_in[lev, half, 0]
        return jnp.concatenate([upper, lower], axis=0)

    class Place:
        def __init__(self, piece, buf, out):
            tz, tx = t_z.at[piece], t_x.at[piece]
            self.buf, self.out, self.tz, self.tx = buf, out, tz, tx
            self.z_base, self.x_base = take(4), take(4)
            self.got_z, self.got_x = take(1), take(1)
            self.via_z = copy(
                buf.at[up], tz.at[k], dev(k=h), recv=self.z_base + ring(k, 4 - h), start=False
            )
            self.via_x = copy(
                buf.at[dn], tx.at[h], dev(h=k), recv=self.x_base + ring(h, 4 - k), start=False
            )
            self.on_z, self.on_x = [], []
            for o in (1, 2, 3):
                v = ring(k, o)
                self.on_z.append(
                    copy(tz.at[v], out.at[up], dev(h=v), recv=self.got_z, start=False)
                )
                self.on_x.append(
                    copy(tx.at[v], out.at[dn], dev(k=v), recv=self.got_x, start=False)
                )

        def begin_x(self):
            @pl.when(h != k)
            def _():
                self.via_x.start()

            @pl.when(h == k)
            def _():
                self.out[...] = self.buf[...]

        def begin_z(self):
            @pl.when(h != k)
            def _():
                self.via_z.start()

        def pass_x(self):
            @pl.when(h == k)
            def _():
                for o in (2, 1, 3):
                    arrival(self.tx.at[ring(k, o)], self.x_base + o).wait_recv()
                    self.on_x[o - 1].start()

        def pass_z(self):
            @pl.when(h == k)
            def _():
                for o in (2, 1, 3):
                    arrival(self.tz.at[ring(k, o)], self.z_base + o).wait_recv()
                    self.on_z[o - 1].start()

        def finish(self):
            @pl.when(h != k)
            def _():
                self.via_z.wait_send()
                self.via_x.wait_send()
                arrival(self.out.at[up], self.got_z).wait_recv()
                arrival(self.out.at[dn], self.got_x).wait_recv()

            @pl.when(h == k)
            def _():
                for op in self.on_z + self.on_x:
                    op.wait_send()

    left, right = pl.ds(0, 128), pl.ds(128, 128)
    place_20 = Place(0, x2.at[:, left], u2.at[:, left])
    place_21 = Place(1, x2.at[:, right], u2.at[:, right])
    place_10 = Place(2, x1.at[:, left], u1.at[:, left])
    place_11 = Place(3, x1.at[:, right], u1.at[:, right])

    def x2_half(half, ops):
        value = -total(0, half, ops)
        x2[:, 128 * half : 128 * half + 128] = value
        x2all[half, n] = value

    duo = product(0, 0, 0)
    for op in fa0:
        op.wait_recv()
    split_a(0, 3)
    add_cores(duo + product(0, 0, 1))
    rs00 = reduce_start(0, 0)
    fa1 = forward_a(1, a1)
    share(0)
    w1.wait_recv()
    p1 = send_pair(1)
    f1 = forward_l(1, o1, w)
    split_l(1, theirs)
    split_l(1, ml + w)
    split_l(1, mr + w)
    relay(0, 0, rs00)
    e1 = forward_l(1, p1, 1 - w)

    @pl.when(h != k)
    def _():
        lp_ops[0].wait_recv()

    lp_w = copy(lpn.at[rows32], lpn.at[rows32], pair)
    split_l(1, ml + 1 - w)
    split_l(1, mr + 1 - w)
    a1[2].wait_recv()
    split_a(1, 1)
    a1[3].wait_recv()
    split_a(1, 2)
    duo = product(0, 1, 0)
    for op in f1:
        op.wait_recv()
    split_l(1, mf + w)
    x2_half(0, rs00)
    place_20.begin_x()
    place_20.begin_z()
    for op in fa1:
        op.wait_recv()
    split_a(1, 3)
    add_cores(duo + product(0, 1, 1))
    rs01 = reduce_start(0, 1)
    for op in e1:
        op.wait_recv()
    split_l(1, mf + 1 - w)

    def gather_start(buf):
        return copy(buf.at[n], buf.at[n], hr), copy(buf.at[n], buf.at[n], hl), copy(
            buf.at[n], buf.at[n], sib
        )

    def gather_mid(buf, ops):
        left, right = 2 * ring(h, -1) + c, 2 * ring(h, 1) + c
        ops[0].wait_recv()
        one = copy(buf.at[left, up], buf.at[left, up], hr)
        sib_l = copy(buf.at[left], buf.at[left], sib)
        ops[1].wait_recv()
        two = copy(buf.at[right, dn], buf.at[right, dn], hl)
        sib_r = copy(buf.at[right], buf.at[right], sib)
        return one, two, ops[2], sib_l, sib_r

    def gather_end(buf, ops):
        opp = 2 * ring(h, 2) + c
        ops[0].wait_recv()
        ops[1].wait_recv()
        last = copy(buf.at[opp], buf.at[opp], sib)
        for op in ops[2:]:
            op.wait_recv()
        last.wait_recv()

    x20 = gather_start(x2all.at[0])
    lp_w.wait_recv()
    lp_y = [copy(lpn.at[rows64], lpn.at[rows64], dev(y=ring(y, o))) for o in (1, 2, 3)]
    duo = product(1, 0, 0)
    add_cores(duo + product(1, 0, 1))
    rs10 = reduce_start(1, 0)
    relay(0, 1, rs01)
    duo = product(1, 1, 0)
    add_cores(duo + product(1, 1, 1))
    rs11 = reduce_start(1, 1)
    share(1)
    place_20.pass_x()
    place_20.pass_z()
    x20 = gather_mid(x2all.at[0], x20)
    relay(1, 0, rs10)

    own8 = pl.ds(pl.multiple_of(zi * 8, 8), 8)

    class Chain:
        def __init__(self, red, ry, yr, rz, zr, gz, fin):
            self.bufs = (red, ry, yr, rz, zr, gz, fin)

        def y_start(self):
            red, ry = self.bufs[:2]
            self.ops = []
            for o in (1, 2, 3):
                to = ring(y, o)
                part = pl.ds(pl.multiple_of(to * 64, 64), 64)
                self.ops.append(copy(red.at[:, part], ry.at[o - 1], dev(y=to)))

        def z_start(self):
            red, ry, yr, rz = self.bufs[:4]
            acc = red[:, rows64, :]
            for o in range(3):
                self.ops[o].wait_recv()
                acc = acc + ry[o]
            yr[...] = acc
            self.ops = []
            for o in range(1, 8):
                to = ring(zi, o, 8)
                part = pl.ds(pl.multiple_of(to * 8, 8), 8)
                self.ops.append(copy(yr.at[:, part], rz.at[o - 1], zdev(to)))

        def plane_start(self, less=None):
            yr, rz, zr, gz = self.bufs[2:6]
            acc = yr[:, own8, :]
            for o in range(7):
                self.ops[o].wait_recv()
                acc = acc + rz[o]
            zr[...] = acc if less is None else acc - less[None]
            self.base = take(8)
            self.sends = []
            for v in (0, 1):
                op = copy(
                    zr, gz.at[:, own8], dev(k=h, w=v), recv=self.base + zi, start=False
                )
                self.sends.append(op)

                @pl.when(2 * h + v != zi)
                def _(op=op):
                    op.start()

        def x_send(self):
            zr, gz = self.bufs[4:6]
            got = ids[0]
            self.spread = [
                copy(gz, gz, dev(h=ring(h, o)), recv=got, start=False) for o in (1, 2, 3)
            ]

            @pl.when(h == k)
            def _():
                gz[:, own8, :] = zr[...]
                for o in range(1, 8):
                    frm = ring(zi, o, 8)
                    part = pl.ds(pl.multiple_of(frm * 8, 8), 8)
                    arrival(gz.at[:, part], self.base + frm).wait_recv()
                for op in self.spread:
                    op.start()

        def x_recv(self):
            @pl.when(h != k)
            def _():
                self.spread[0].wait_recv()

        def y_spread(self):
            gz, fin = self.bufs[5:]
            self.ops = [copy(gz, fin.at[:, rows64], dev(y=ring(y, o))) for o in (1, 2, 3)]
            fin[:, rows64, :] = gz[...]

        def finish(self):
            for op in self.ops:
                op.wait_recv()

        def drain(self):
            for v in (0, 1):

                @pl.when(2 * h + v != zi)
                def _(v=v):
                    self.sends[v].wait_send()

            @pl.when(h == k)
            def _():
                for op in self.spread:
                    op.wait_send()

    sum_g = Chain(red_g, ry_g, yr_g, rz_g, zr_g, gz_g, fin_g)
    sum_f = Chain(red_f, ry_f, yr_f, rz_f, zr_f, gz_f, fin_f)
    sum_s = Chain(red_s, ry_s, yr_s, rz_s, zr_s, gz_s, fin_s)
    x2_half(1, rs01)
    place_21.begin_x()
    place_21.begin_z()
    x21 = gather_start(x2all.at[1])
    red_g[0] = mm(lloc[0], x2[...], NT)
    sum_g.y_start()
    gather_end(x2all.at[0], x20)
    x21 = gather_mid(x2all.at[1], x21)
    relay(1, 1, rs11)
    sum_g.z_start()
    for op in lp_y:
        op.wait_recv()
    parent = par[n]
    lp_h, lp_l = split(lpn[...])
    d2c.wait_recv()
    here = jnp.where(parent == r, 1.0, 0.0)
    beside = jnp.where(parent == 2 * k + oc, 1.0, 0.0)
    own_rows = dot3(*split(d2[0, rows32] * here + d2s[0, rows32] * beside), lp_h, lp_l, NT)
    gather_end(x2all.at[1], x21)
    x2p = jnp.concatenate([x2all[0, parent], x2all[1, parent]], axis=1)
    red_f[0] = mm(x2p, lloc[1], NT)
    red_f[0, rows32] += own_rows
    sum_f.y_start()
    correction = dot3(lp_h, lp_l, *split(x2p))
    sum_g.plane_start()
    g_all[n] = zr_g[0]
    slices = [copy(g_all.at[n], g_all.at[n], sib)]
    for o in (1, 2, 3):
        for core in (c, oc):
            slices.append(copy(g_all.at[n], g_all.at[n], dev(h=ring(h, o), c=core)))
    sum_f.z_start()
    sum_g.x_send()
    x1[:, 0:128] = -total(1, 0, rs10) - correction[:, 0:128]
    place_10.begin_x()
    place_10.begin_z()
    near_s = mm(lloc[1, :, 0:128], x1[:, 0:128], NT)
    x1[:, 128:256] = -total(1, 1, rs11) - correction[:, 128:256]
    red_s[0] = near_s + mm(lloc[1, :, 128:256], x1[:, 128:256], NT)
    sum_s.y_start()
    place_11.begin_x()
    place_21.pass_x()
    place_21.pass_z()
    for op in slices:
        op.wait_recv()
    sum_f.plane_start(dot3(*split(g_all[parent]), lp_h, lp_l, NT))
    sum_g.x_recv()
    sum_g.y_spread()
    sum_s.z_start()
    sum_f.x_send()
    sum_s.plane_start()
    place_10.pass_x()
    place_11.begin_z()
    place_11.pass_x()
    sum_s.x_send()
    sum_f.x_recv()
    sum_f.y_spread()
    sum_g.finish()
    g2o[...] = d2[0] - fin_g[0]
    sum_s.x_recv()
    sum_s.y_spread()
    place_10.pass_z()
    place_11.pass_z()
    sum_f.finish()
    pb = -fin_f[0]
    pbo[...] = pb
    update = d1[0] - mm(lpt[...], pb)
    sum_s.finish()
    g1o[...] = update - fin_s[0]
    place_20.finish()
    for move in (place_21, place_10, place_11):
        move.finish()

    for chain in (sum_g, sum_f, sum_s):
        chain.drain()

    @pl.when(h == k)
    def _():
        for op in lp_ops:
            op.wait_send()

    @pl.when(c == cy)
    def _():
        for op in l_ops:
            op.wait_send()

    for op in pending:
        op.wait_send()
    assert ids[0] <= SEMS


def settle(*refs):
    held, in_sem, out_sem = refs[10:]
    loads, stores = [], []
    for num in range(5):
        loads.append(pltpu.make_async_copy(refs[num], held.at[num], in_sem.at[num]))
        loads[-1].start()
    for num in range(5):
        dst = refs[5 + num]
        to = dst.at[0] if len(dst.shape) == 3 else dst
        stores.append(pltpu.make_async_copy(held.at[num], to, out_sem.at[num]))
        loads[num].wait()
        stores[-1].start()
    for op in stores:
        op.wait()


def per_device(
    inverse_anc,
    lower_two,
    pattern_two,
    widths_two,
    dinv_two,
    lower_one,
    pattern_one,
    widths_one,
    parent_one,
    lower_par,
    dinv_one,
):
    vmem = pl.BlockSpec(memory_space=pltpu.VMEM)
    smem = pl.BlockSpec(memory_space=pltpu.SMEM)
    square = jax.ShapeDtypeStruct((B, B), F32)
    cube = jax.ShapeDtypeStruct((1, B, B), F32)

    def chain(count):
        return [
            pltpu.VMEM((count, B, B), F32),
            pltpu.VMEM((3, count, 64, B), F32),
            pltpu.VMEM((count, 64, B), F32),
            pltpu.VMEM((7, count, 8, B), F32),
            pltpu.VMEM((count, 8, B), F32),
            pltpu.VMEM((count, 64, B), F32),
            pltpu.VMEM((count, B, B), F32),
        ]

    outs = pl.pallas_call(
        kernel,
        out_shape=[square] * 5,
        in_specs=[smem] * 5 + [pl.BlockSpec(memory_space=pl.ANY)] + [vmem] * 5,
        out_specs=[vmem] * 5,
        scratch_shapes=[
            pltpu.VMEM((1024, B), F32),
            pltpu.VMEM((3, 2, 1024, 128), F32),
            pltpu.VMEM((2, 64, 1024), F32),
            pltpu.VMEM((2, 8, 64, 1024), F32),
            pltpu.VMEM((2, 8, 64, 1024), BF16),
            pltpu.VMEM((2, 8, 64, 1024), BF16),
            pltpu.VMEM((2, 2, 1024, B), BF16),
            pltpu.VMEM((2, 2, 1024, B), BF16),
            pltpu.VMEM((2, 2, 4, 2, B, 128), F32),
            pltpu.VMEM((2, 2, 4, B, 128), F32),
            pltpu.VMEM((2, 2, 2, 128, 128), F32),
            pltpu.VMEM((2, 2, 2, 128, 128), F32),
            pltpu.VMEM((2, 2, 2, 128, 128), F32),
            pltpu.VMEM((2, 2, 2, 128, 128), F32),
            pltpu.VMEM((2, B, B), F32),
            pltpu.VMEM((2, B, B), F32),
            pltpu.VMEM((B, B), F32),
            pltpu.VMEM((B, B), F32),
            pltpu.VMEM((1, B, B), F32),
            pltpu.VMEM((2, 8, B, 128), F32),
            pltpu.VMEM((B, B), F32),
            pltpu.VMEM((B, B), F32),
            pltpu.VMEM((4, 4, 128, 128), F32),
            pltpu.VMEM((4, 4, 128, 128), F32),
            pltpu.VMEM((8, 8, B), F32),
            *chain(1),
            *chain(1),
            *chain(1),
            pltpu.SemaphoreType.DMA((SEMS,)),
            pltpu.SemaphoreType.DMA((SEMS,)),
            pltpu.SemaphoreType.DMA,
        ],
        compiler_params=pltpu.CompilerParams(
            collective_id=0, has_side_effects=True, vmem_limit_bytes=56 * 1024 * 1024
        ),
    )(
        parent_one,
        widths_two,
        widths_one,
        pattern_two.T,
        pattern_one.T,
        inverse_anc,
        lower_two.T,
        lower_one.T,
        lower_par,
        dinv_two,
        dinv_one,
    )
    u2, g2, u1, pb, g1 = pl.pallas_call(
        settle,
        out_shape=[square, cube, square, cube, cube],
        in_specs=[pl.BlockSpec(memory_space=pl.ANY)] * 5,
        out_specs=[pl.BlockSpec(memory_space=pl.ANY)] * 5,
        scratch_shapes=[
            pltpu.VMEM((5, B, B), F32),
            pltpu.SemaphoreType.DMA((5,)),
            pltpu.SemaphoreType.DMA((5,)),
        ],
    )(outs[0], outs[2], outs[1], outs[3], outs[4])
    return u2, g2, u1, pb, g1


def solution(mesh):
    in_specs = (
        P("prow", "pcol"),
        P("prow", "pcol"),
        P(),
        P(),
        P("prow", None, None),
        P("prow", "pcol"),
        P(),
        P(),
        P(),
        P("prow", None, None),
        P("prow", None, None),
    )
    out_specs = (
        P("prow", "pcol"),
        P("prow", None, None),
        P("prow", "pcol"),
        P("prow", None, None),
        P("prow", None, None),
    )
    return jax.shard_map(
        per_device, mesh=mesh, in_specs=in_specs, out_specs=out_specs, check_vma=False
    )
```
